32 devices in a mesh: dp: 4 (over x, core), row: 2 (over y), col: 4 (over z).
Axes of the slice: x: 2, y: 2, z: 4, core: 2. Of those that a mesh axis runs over, the one named last changes fastest.
Arguments:
- layer_input: bfloat16 [4096, 1024], P(('dp', 'col'), 'row'), may hold values from -6 to 6
- lengths: int32 [8], P('dp'), may hold values from 1 to 512, as said below
- attend_weight: bfloat16 [1024, 3072], P('row', 'col'), may hold values from -0.1875 to 0.1875
- attend_bias: float32 [16, 128], P('col'), may hold values from -0.6 to 0.6
- mixer_weight: bfloat16 [1024, 1024], P('col', 'row'), may hold values from -1.5 to 1.5
- mixer_bias: float32 [1024], P('row'), may hold values from -3 to 3
- first_gain: float32 [1024], P('row'), may hold values from 0.1 to 1.9
- first_shift: float32 [1024], P('row'), may hold values from -3 to 3
- widen_weight: bfloat16 [1024, 4096], P('row', 'col'), may hold values from -0.1875 to 0.1875
- widen_bias: float32 [4096], P('col'), may hold values from -3 to 3
- narrow_weight: bfloat16 [4096, 1024], P('col', 'row'), may hold values from -0.09375 to 0.09375
- narrow_bias: float32 [1024], P('row'), may hold values from -3 to 3
- second_gain: float32 [1024], P('row'), may hold values from 0.1 to 1.9
- second_shift: float32 [1024], P('row'), may hold values from -3 to 3
- cotangent: bfloat16 [4096, 1024], P(('dp', 'col'), 'row'), may hold values from -6 to 6
Outputs:
- layer_output: bfloat16 [4096, 1024], P(('dp', 'col'), 'row')
- input_gradient: float32 [4096, 1024], P(('dp', 'col'), 'row')
- attend_weight_gradient: float32 [1024, 3072], P('row', 'col')
- attend_bias_gradient: float32 [16, 128], P('col')
- mixer_weight_gradient: float32 [1024, 1024], P('col', 'row')
- mixer_bias_gradient: float32 [1024], P('row')
- first_gain_gradient: float32 [1024], P('row')
- first_shift_gradient: float32 [1024], P('row')
- widen_weight_gradient: float32 [1024, 4096], P('row', 'col')
- widen_bias_gradient: float32 [4096], P('col')
- narrow_weight_gradient: float32 [4096, 1024], P('col', 'row')
- narrow_bias_gradient: float32 [1024], P('row')
- second_gain_gradient: float32 [1024], P('row')
- second_shift_gradient: float32 [1024], P('row')
The draws below stay inside these ranges and needn't reach their ends.
Inputs may be any that keep to these rules, and one draw needn't show every extreme that they name: lengths[s] is the length of the sequence in slot s; a replica's 2 slots are consecutive entries; some slot holds the full 512 rows.
All inputs are finite; a program needn't handle non-finite values.
Results may differ from the reference program's by a relative error of at most 0.015.
Values may be sent and summed in bfloat16 or wider, within the bound.
A program may use at most 128 MiB of HBM per device.

```python
import jax
import jax.numpy as jnp
from jax import lax

D = 1024
H = 16
HD = 64
FF = 4096
SEQ = 512
SLOTS = 2
ROWS_REP = 1024
TOKENS = 4096
N_DP = 4


def draw_lengths(key, part):
    key = jax.random.fold_in(key, 11)
    gap_key, raw_key, full_key = jax.random.split(key, 3)
    replicas = TOKENS // ROWS_REP
    gap_draw = jax.random.randint(gap_key, (replicas, 1), 0, SEQ * 3 // 4 + 1)
    raw_draw = jax.random.randint(raw_key, (replicas, SLOTS), 0, SEQ)
    flat_lengths = (SEQ - raw_draw * gap_draw // SEQ).reshape(replicas * SLOTS)
    chosen = jax.random.randint(full_key, (), 0, replicas * SLOTS)
    return jnp.where(jnp.arange(replicas * SLOTS) == chosen, SEQ, flat_lengths).astype(jnp.int32)


def levels(key, extent, cuts, smallest, largest):
    def one(position, parts):
        draws = jax.random.uniform(jax.random.fold_in(jax.random.fold_in(key, 6), position), (parts,), jnp.float32, smallest / len(cuts), largest / len(cuts))
        return jnp.repeat(jnp.exp(draws), extent[position] // parts).reshape((-1,) + (1,) * (len(extent) - position - 1))

    loudness = one(*cuts[0])
    for cut in cuts[1:]:
        loudness = loudness * one(*cut)
    return loudness


def bell_draw(key, extent, scale, most, pieces=(), held_as=jnp.bfloat16):
    level = levels(key, extent, pieces, -0.22, 0.18) if pieces else 1.0
    values = jax.random.normal(key, extent, jnp.float32) * scale * level
    return jnp.minimum(jnp.maximum(values, -most), most).astype(held_as)


def setup_inputs(seed: int = 0) -> dict:
    streams_of = jax.random.split(jax.random.key(seed), 16)
    return {
        "layer_input": bell_draw(streams_of[0], (TOKENS, D), 1.0, 6.0, ((0, 16), (1, 2))),
        "lengths": draw_lengths(jax.random.fold_in(streams_of[15], 71), 0),
        "attend_weight": bell_draw(streams_of[2], (D, 3 * D), D ** -0.5, 0.1875, ((0, 2), (1, 4))),
        "attend_bias": bell_draw(streams_of[3], (H, 2 * HD), 0.1, 0.6, ((0, 4),), jnp.float32),
        "mixer_weight": bell_draw(streams_of[4], (D, D), (D // 64) ** -0.5, 1.5, ((0, 4), (1, 2))),
        "mixer_bias": bell_draw(streams_of[5], (D,), 0.5, 3.0, ((0, 2),), jnp.float32),
        "first_gain": jnp.clip(1.0 + 0.18 * jax.random.normal(streams_of[6], (D,), jnp.float32), 0.1, 1.9),
        "first_shift": bell_draw(streams_of[7], (D,), 0.5, 3.0, ((0, 2),), jnp.float32),
        "widen_weight": bell_draw(streams_of[8], (D, FF), D ** -0.5, 0.1875, ((0, 2), (1, 4))),
        "widen_bias": bell_draw(streams_of[9], (FF,), 0.5, 3.0, ((0, 4),), jnp.float32),
        "narrow_weight": bell_draw(streams_of[10], (FF, D), FF ** -0.5, 0.09375, ((0, 4), (1, 2))),
        "narrow_bias": bell_draw(streams_of[11], (D,), 0.5, 3.0, ((0, 2),), jnp.float32),
        "second_gain": jnp.clip(1.0 + 0.18 * jax.random.normal(streams_of[12], (D,), jnp.float32), 0.1, 1.9),
        "second_shift": bell_draw(streams_of[13], (D,), 0.5, 3.0, ((0, 2),), jnp.float32),
        "cotangent": bell_draw(streams_of[14], (TOKENS, D), 1.0, 6.0, ((0, 16), (1, 2))),
    }


@jax.custom_vjp
def low(v):
    return lax.optimization_barrier(v.astype(jnp.bfloat16)).astype(jnp.float32)

@jax.custom_vjp
def low_back(v):
    return v

def low_keep(v):
    return (low(v), None)

def low_pass(kept, grad):
    return (grad,)

def back_keep(v):
    return (v, None)

def back_low(kept, grad):
    return (low(grad),)
low.defvjp(low_keep, low_pass)
low_back.defvjp(back_keep, back_low)
EPSILON = 1e-12
MASKED = -1e+30
PRECISE = lax.Precision.HIGHEST

def matmul(left_side, right_side):
    return jnp.dot(left_side, right_side, precision=PRECISE, preferred_element_type=jnp.float32)

def normalize(summed, gain_row, shift_row):
    average = lax.optimization_barrier(jnp.mean(summed, axis=-1, keepdims=True))
    centred = summed - average
    variance = lax.optimization_barrier(jnp.mean(centred * centred, axis=-1, keepdims=True))
    return centred * lax.rsqrt(variance + EPSILON) * gain_row + shift_row

def attend_slot(slot_item):
    query_part, key_part, value_part, length = slot_item
    scores = jnp.einsum('qhd,khd->hqk', query_part, key_part, precision=PRECISE) * HD ** (-0.5)
    valid_keys = jnp.arange(SEQ) < length
    scores = low_back(jnp.where(valid_keys[None, None, :], scores, MASKED))
    row_top = lax.optimization_barrier(jnp.max(scores, axis=2, keepdims=True))
    exponent = jnp.exp(scores - row_top)
    probabilities = low(exponent / lax.optimization_barrier(jnp.sum(exponent, axis=2, keepdims=True)))
    return jnp.einsum('hqk,khd->qhd', probabilities, value_part, precision=PRECISE)

def forward(inputs, slot_lengths, attend_weight, attend_bias, mixer_weight, mixer_bias, first_gain, first_shift, widen_weight, widen_bias, narrow_weight, narrow_bias, second_gain, second_shift):
    bias_full = jnp.concatenate([attend_bias[:, :HD], jnp.zeros((H, HD), jnp.float32), attend_bias[:, HD:]], axis=1).reshape(3 * D)
    packed = low(low_back(matmul(inputs, attend_weight) + bias_full))
    split_heads = packed.reshape(SLOTS, SEQ, H, 3, HD)
    mixed = lax.map(jax.checkpoint(attend_slot), (split_heads[:, :, :, 0], split_heads[:, :, :, 1], split_heads[:, :, :, 2], slot_lengths))
    mixed = low(low_back(mixed.reshape(ROWS_REP, D)))
    attended = low_back(matmul(mixed, mixer_weight) + mixer_bias)
    first = normalize(inputs + attended, first_gain, first_shift)
    widened = low_back(matmul(low(first), widen_weight) + widen_bias)
    active = low(jax.nn.gelu(widened, approximate=False))
    narrowed = low_back(matmul(active, narrow_weight) + narrow_bias)
    return normalize(first + narrowed, second_gain, second_shift)

def reference(layer_input, lengths, attend_weight, attend_bias, mixer_weight, mixer_bias, first_gain, first_shift, widen_weight, widen_bias, narrow_weight, narrow_bias, second_gain, second_shift, cotangent):
    weights = tuple((weight_item.astype(jnp.float32) for weight_item in (attend_weight, attend_bias, mixer_weight, mixer_bias, first_gain, first_shift, widen_weight, widen_bias, narrow_weight, narrow_bias, second_gain, second_shift)))
    rows_all = layer_input.astype(jnp.float32).reshape(N_DP, ROWS_REP, D)
    lengths_all = lengths.reshape(N_DP, SLOTS)
    upstream_all = cotangent.astype(jnp.float32).reshape(N_DP, ROWS_REP, D)

    def replica_step(totals, replica_item):
        replica_rows, replica_lengths, replica_upstream = replica_item

        def run_layer(inputs, *params):
            return forward(inputs, replica_lengths, *params)
        output, pullback = jax.vjp(run_layer, replica_rows, *weights)
        positions = jnp.arange(ROWS_REP) % SEQ
        owners = jnp.arange(ROWS_REP) // SEQ
        valid_rows = positions < replica_lengths[owners]
        gradients = pullback(jnp.where(valid_rows[:, None], replica_upstream, 0.0))
        totals = tuple((total_item + grad_item for total_item, grad_item in zip(totals, gradients[1:])))
        return (totals, (output.astype(jnp.bfloat16), gradients[0]))
    zeros_init = tuple((jnp.zeros_like(weight_item) for weight_item in weights))
    totals, (outputs, input_grads) = lax.scan(replica_step, zeros_init, (rows_all, lengths_all, upstream_all))
    return (outputs.reshape(TOKENS, D), input_grads.reshape(TOKENS, D), totals[0], totals[1], totals[2], totals[3], totals[4], totals[5], totals[6], totals[7], totals[8], totals[9], totals[10], totals[11])
```

```python
import functools

import jax
import jax.numpy as jnp
from jax import lax
from jax.experimental import pallas as pl
from jax.experimental.pallas import tpu as pltpu
from jax.sharding import PartitionSpec as P

D = 1024
HD = 64


EPSILON = 1e-12
MASKED = -1e30


def product(left_side, right_side):
    return jnp.dot(left_side, right_side, preferred_element_type=jnp.float32)


def inner_rows(left_side, right_side):
    return lax.dot_general(
        left_side, right_side, (((0,), (0,)), ((), ())), preferred_element_type=jnp.float32
    )


def outer_back(left_side, right_side):
    return lax.dot_general(
        left_side, right_side, (((1,), (1,)), ((), ())), preferred_element_type=jnp.float32
    )


def gelu_exact(values):
    return jax.nn.gelu(values, approximate=False)


VMEM_BYTES = 32 * 1024 * 1024


def greet(me, count):
    barrier = pltpu.get_barrier_semaphore()

    @pl.when(me > 0)
    def _():
        pl.semaphore_signal(
            barrier, inc=1, device_id={"col": me - 1}, device_id_type=pl.DeviceIdType.MESH
        )

    @pl.when(me < count - 1)
    def _():
        pl.semaphore_signal(
            barrier, inc=1, device_id={"col": me + 1}, device_id_type=pl.DeviceIdType.MESH
        )

    inner = (me > 0) & (me < count - 1)

    @pl.when(inner)
    def _():
        pl.semaphore_wait(barrier, 2)

    @pl.when(jnp.logical_not(inner))
    def _():
        pl.semaphore_wait(barrier, 1)


def chain_gather(count, block_ref, out_ref, send_sem, recv_sem):
    me = lax.axis_index("col")
    greet(me, count)
    rows = block_ref.shape[0]

    def span(owner):
        return out_ref.at[pl.ds(pl.multiple_of(owner * rows, rows), rows)]

    def hop(source, owner, target, way, step):
        return pltpu.make_async_remote_copy(
            src_ref=source,
            dst_ref=span(owner),
            send_sem=send_sem.at[way, step],
            recv_sem=recv_sem.at[way, step],
            device_id={"col": target},
            device_id_type=pl.DeviceIdType.MESH,
        )

    for step in range(count - 1):

        @pl.when((me < count - 1) & (me - step >= 0))
        def _():
            source = block_ref if step == 0 else span(me - step)
            hop(source, me - step, me + 1, 0, step).start()

        @pl.when((me > 0) & (me + step <= count - 1))
        def _():
            source = block_ref if step == 0 else span(me + step)
            hop(source, me + step, me - 1, 1, step).start()

        if step == 0:
            out_ref[pl.ds(pl.multiple_of(me * rows, rows), rows), :] = block_ref[...]

        @pl.when(me - step - 1 >= 0)
        def _():
            hop(span(me - step - 1), me - step - 1, me, 0, step).wait_recv()

        @pl.when(me + step + 1 <= count - 1)
        def _():
            hop(span(me + step + 1), me + step + 1, me, 1, step).wait_recv()

    for step in range(count - 1):

        @pl.when((me < count - 1) & (me - step >= 0))
        def _():
            hop(span(me - step), me - step, me + 1, 0, step).wait_send()

        @pl.when((me > 0) & (me + step <= count - 1))
        def _():
            hop(span(me + step), me + step, me - 1, 1, step).wait_send()


def gather_tokens(block):
    count = lax.axis_size("col")
    rows, width = block.shape
    return pl.pallas_call(
        functools.partial(chain_gather, count),
        out_shape=jax.ShapeDtypeStruct((count * rows, width), block.dtype),
        in_specs=[pl.BlockSpec(memory_space=pltpu.VMEM)],
        out_specs=pl.BlockSpec(memory_space=pltpu.VMEM),
        scratch_shapes=[
            pltpu.SemaphoreType.DMA((2, count - 1)),
            pltpu.SemaphoreType.DMA((2, count - 1)),
        ],
        compiler_params=pltpu.CompilerParams(
            collective_id=0, has_side_effects=True, vmem_limit_bytes=VMEM_BYTES
        ),
        cost_estimate=pl.CostEstimate(
            flops=0, bytes_accessed=30 * 1024 * 1024, transcendentals=0
        ),
        name="chain_gather",
    )(block)


def chain_scatter(count, part_ref, out_ref, held, sent, send_sem, recv_sem):
    me = lax.axis_index("col")
    greet(me, count)
    rows = out_ref.shape[0]

    def mine(owner):
        return part_ref[pl.ds(pl.multiple_of(owner * rows, rows), rows), :].astype(jnp.float32)

    def hop(way, owner, target):
        return pltpu.make_async_remote_copy(
            src_ref=sent.at[way, owner],
            dst_ref=held.at[way, owner],
            send_sem=send_sem.at[way, owner],
            recv_sem=recv_sem.at[way, owner],
            device_id={"col": target},
            device_id_type=pl.DeviceIdType.MESH,
        )

    for step in range(count - 1):
        for way, owner, inside in (
            (0, count - 1 - step, me < count - 1 - step),
            (1, step, me > step),
        ):
            first = me == 0 if way == 0 else me == count - 1
            target = me + 1 if way == 0 else me - 1

            @pl.when(inside & first)
            def _():
                sent[way, owner] = mine(owner).astype(sent.dtype)
                hop(way, owner, target).start()

            @pl.when(inside & jnp.logical_not(first))
            def _():
                hop(way, owner, target).wait_recv()
                total = mine(owner) + held[way, owner].astype(jnp.float32)
                sent[way, owner] = total.astype(sent.dtype)
                hop(way, owner, target).start()

    out_ref[...] = mine(me)

    @pl.when(me > 0)
    def _():
        hop(0, me, me).wait_recv()
        out_ref[...] += held[0, me].astype(jnp.float32)

    @pl.when(me < count - 1)
    def _():
        hop(1, me, me).wait_recv()
        out_ref[...] += held[1, me].astype(jnp.float32)

    for step in range(count - 1):
        for way, owner, inside in (
            (0, count - 1 - step, me < count - 1 - step),
            (1, step, me > step),
        ):

            @pl.when(inside)
            def _():
                hop(way, owner, me).wait_send()


def scatter_tokens(part):
    count = lax.axis_size("col")
    rows, width = part.shape[0] // count, part.shape[1]
    return pl.pallas_call(
        functools.partial(chain_scatter, count),
        out_shape=jax.ShapeDtypeStruct((rows, width), jnp.float32),
        in_specs=[pl.BlockSpec(memory_space=pltpu.VMEM)],
        out_specs=pl.BlockSpec(memory_space=pltpu.VMEM),
        scratch_shapes=[
            pltpu.VMEM((2, count, rows, width), jnp.bfloat16),
            pltpu.VMEM((2, count, rows, width), jnp.bfloat16),
            pltpu.SemaphoreType.DMA((2, count)),
            pltpu.SemaphoreType.DMA((2, count)),
        ],
        compiler_params=pltpu.CompilerParams(
            collective_id=1, has_side_effects=True, vmem_limit_bytes=VMEM_BYTES
        ),
        cost_estimate=pl.CostEstimate(
            flops=0, bytes_accessed=30 * 1024 * 1024, transcendentals=0
        ),
        name="chain_scatter",
    )(part)


def slot_moves(swap):
    col_count = lax.axis_size("col")
    half = col_count // 2
    pairs = []
    for row in range(2):
        for col in range(col_count):
            there = (col // half) * col_count + 2 * (col % half) + (row ^ swap)
            pairs.append((row * col_count + col, there))
    return pairs


def to_slot_rows(stored):
    row, col = lax.axis_index("row"), lax.axis_index("col")
    rows = stored.shape[0] // 2
    landed = []
    for swap in range(2):
        block = lax.dynamic_slice_in_dim(stored, (row ^ swap) * rows, rows, 0)
        landed.append(lax.ppermute(block, ("row", "col"), slot_moves(swap)))
    odd = (col % 2) == 1
    left = jnp.where(odd, landed[1], landed[0])
    right = jnp.where(odd, landed[0], landed[1])
    return jnp.concatenate([left, right], axis=1)


def from_slot_rows(block):
    row, col = lax.axis_index("row"), lax.axis_index("col")
    width = block.shape[1] // 2
    landed = []
    for swap in range(2):
        piece = lax.dynamic_slice_in_dim(block, ((col % 2) ^ swap) * width, width, 1)
        pairs = [(there, here) for here, there in slot_moves(swap)]
        landed.append(lax.ppermute(piece, ("row", "col"), pairs))
    upper = jnp.where(row == 1, landed[1], landed[0])
    lower = jnp.where(row == 1, landed[0], landed[1])
    return jnp.concatenate([upper, lower], axis=0)


def norm_forward(summed, gain_row, shift_row):
    average = jnp.mean(summed, axis=1, keepdims=True)
    centred = summed - average
    variance = jnp.mean(centred * centred, axis=1, keepdims=True)
    inverse = lax.rsqrt(variance + EPSILON)
    normal = centred * inverse
    return (normal * gain_row + shift_row, normal, inverse)


def norm_backward(upstream, normal, inverse, gain_row):
    scaled = upstream * gain_row
    average = jnp.mean(scaled, axis=1, keepdims=True)
    crossed = jnp.mean(scaled * normal, axis=1, keepdims=True)
    return (scaled - average - normal * crossed) * inverse


def slot_scores(query_part, key_part, length):
    scores = jnp.einsum(
        "qhd,khd->hqk", query_part, key_part, preferred_element_type=jnp.float32
    ) * HD ** (-0.5)
    valid_keys = lax.iota(jnp.int32, key_part.shape[0]) < length
    return jnp.where(valid_keys[None, None, :], scores, MASKED)


def slot_forward(slot_item):
    query_part, key_part, value_part, length = slot_item
    scores = slot_scores(query_part, key_part, length)
    row_top = jnp.max(scores, axis=2, keepdims=True)
    exponent = jnp.exp(scores - row_top)
    row_total = jnp.sum(exponent, axis=2, keepdims=True)
    probabilities = (exponent / row_total).astype(jnp.bfloat16)
    mixed = jnp.einsum(
        "hqk,khd->qhd", probabilities, value_part, preferred_element_type=jnp.float32
    )
    return (mixed.astype(jnp.bfloat16), (row_top + jnp.log(row_total))[:, :, 0])


def slot_backward(slot_item):
    query_part, key_part, value_part, length, logsum, grad_heads = slot_item
    probabilities = jnp.exp(slot_scores(query_part, key_part, length) - logsum[:, :, None])
    grad_probs = jnp.einsum(
        "qhd,khd->hqk", grad_heads, value_part, preferred_element_type=jnp.float32
    )
    grad_values = jnp.einsum(
        "hqk,qhd->khd",
        probabilities.astype(jnp.bfloat16),
        grad_heads,
        preferred_element_type=jnp.float32,
    )
    along = jnp.sum(probabilities * grad_probs, axis=2, keepdims=True)
    grad_scores = (probabilities * (grad_probs - along)).astype(jnp.bfloat16)
    grad_query = jnp.einsum(
        "hqk,khd->qhd", grad_scores, key_part, preferred_element_type=jnp.float32
    ) * HD ** (-0.5)
    grad_keys = jnp.einsum(
        "hqk,qhd->khd", grad_scores, query_part, preferred_element_type=jnp.float32
    ) * HD ** (-0.5)
    return jnp.stack([grad_query, grad_keys, grad_values], axis=2)


def weight_total(part, dimension):
    part = lax.psum_scatter(
        part.astype(jnp.bfloat16), "row", scatter_dimension=dimension, tiled=True
    )
    return lax.psum(part, "dp").astype(jnp.float32)


def per_device(
    layer_input,
    lengths,
    attend_weight,
    attend_bias,
    mixer_weight,
    mixer_bias,
    first_gain,
    first_shift,
    widen_weight,
    widen_bias,
    narrow_weight,
    narrow_bias,
    second_gain,
    second_shift,
    cotangent,
):
    row_rank = lax.axis_index("row")
    col_rank = lax.axis_index("col")
    heads_here = attend_bias.shape[0]
    input_block = to_slot_rows(layer_input)
    block_rows = input_block.shape[0]
    length = lax.dynamic_index_in_dim(lengths, row_rank, 0, keepdims=False)
    vectors = jnp.stack(
        [mixer_bias, first_gain, first_shift, narrow_bias, second_gain, second_shift]
    )
    vectors = lax.all_gather(vectors, "row", axis=1, tiled=True)
    mixer_bias, first_gain, first_shift, narrow_bias, second_gain, second_shift = vectors
    attend_weight = lax.all_gather(attend_weight, "row", axis=0, tiled=True)
    mixer_weight = lax.all_gather(mixer_weight, "row", axis=1, tiled=True)
    widen_weight = lax.all_gather(widen_weight, "row", axis=0, tiled=True)
    narrow_weight = lax.all_gather(narrow_weight, "row", axis=1, tiled=True)

    gathered_input = gather_tokens(input_block)
    slot_rows = gathered_input.shape[0]
    bias_full = jnp.concatenate(
        [attend_bias[:, :HD], jnp.zeros((heads_here, HD), jnp.float32), attend_bias[:, HD:]],
        axis=1,
    ).reshape(heads_here * 3 * HD)
    packed = (product(gathered_input, attend_weight) + bias_full).astype(jnp.bfloat16)
    split_heads = packed.reshape(slot_rows, heads_here, 3, HD)
    query_all = split_heads[:, :, 0]
    keys_all = split_heads[:, :, 1]
    values_all = split_heads[:, :, 2]
    mixed, logsum = slot_forward((query_all, keys_all, values_all, length))
    mixed_block = mixed.reshape(slot_rows, heads_here * HD)
    attended = scatter_tokens(product(mixed_block, mixer_weight)) + mixer_bias
    first_out, first_normal, first_inverse = norm_forward(
        input_block.astype(jnp.float32) + attended, first_gain, first_shift
    )
    gathered_first = gather_tokens(first_out.astype(jnp.bfloat16))
    widened = product(gathered_first, widen_weight) + widen_bias
    active, gelu_pull = jax.vjp(gelu_exact, widened)
    active_block = active.astype(jnp.bfloat16)
    narrowed = scatter_tokens(product(active_block, narrow_weight)) + narrow_bias
    second_out, second_normal, second_inverse = norm_forward(
        first_out + narrowed, second_gain, second_shift
    )
    layer_output = from_slot_rows(second_out.astype(jnp.bfloat16))
    positions = col_rank * block_rows + lax.iota(jnp.int32, block_rows)
    upstream = jnp.where(
        (positions < length)[:, None], to_slot_rows(cotangent).astype(jnp.float32), 0.0
    )
    second_gain_part = jnp.sum(upstream * second_normal, axis=0)
    second_shift_part = jnp.sum(upstream, axis=0)
    grad_second = norm_backward(upstream, second_normal, second_inverse, second_gain)
    grad_narrowed = grad_second.astype(jnp.bfloat16)
    narrow_bias_part = jnp.sum(grad_narrowed, axis=0, dtype=jnp.float32)
    grad_narrow_block = gather_tokens(grad_narrowed)
    narrow_total = weight_total(inner_rows(active_block, grad_narrow_block), 1)
    grad_active = outer_back(grad_narrow_block, narrow_weight)
    grad_widened = gelu_pull(grad_active)[0].astype(jnp.bfloat16)
    widen_bias_part = jnp.sum(grad_widened, axis=0, dtype=jnp.float32)
    grad_first = scatter_tokens(outer_back(grad_widened, widen_weight)) + grad_second
    widen_total = weight_total(inner_rows(gathered_first, grad_widened), 0)
    first_gain_part = jnp.sum(grad_first * first_normal, axis=0)
    first_shift_part = jnp.sum(grad_first, axis=0)
    grad_attended = norm_backward(grad_first, first_normal, first_inverse, first_gain)
    grad_mix = grad_attended.astype(jnp.bfloat16)
    mixer_bias_part = jnp.sum(grad_mix, axis=0, dtype=jnp.float32)
    grad_mixer_block = gather_tokens(grad_mix)
    mixer_total = weight_total(inner_rows(mixed_block, grad_mixer_block), 1)
    grad_mixed = outer_back(grad_mixer_block, mixer_weight).astype(jnp.bfloat16)
    grad_heads = grad_mixed.reshape(slot_rows, heads_here, HD)
    grad_slots = slot_backward((query_all, keys_all, values_all, length, logsum, grad_heads))
    grad_packed = grad_slots.reshape(slot_rows, heads_here * 3 * HD).astype(jnp.bfloat16)
    packed_sums = jnp.sum(grad_packed, axis=0, dtype=jnp.float32).reshape(heads_here, 3, HD)
    attend_bias_part = jnp.concatenate([packed_sums[:, 0], packed_sums[:, 2]], axis=1)
    attend_total = weight_total(inner_rows(gathered_input, grad_packed), 0)
    input_gradient = scatter_tokens(outer_back(grad_packed, attend_weight)) + grad_attended
    input_gradient = from_slot_rows(input_gradient)
    column_totals = lax.psum((attend_bias_part, widen_bias_part), ("dp", "row"))
    vector_parts = jnp.stack(
        [
            mixer_bias_part,
            first_gain_part,
            first_shift_part,
            narrow_bias_part,
            second_gain_part,
            second_shift_part,
        ]
    )
    half = vector_parts.shape[1] // 2
    vector_totals = lax.dynamic_slice_in_dim(
        lax.psum(vector_parts, ("dp", "row", "col")), row_rank * half, half, 1
    )
    return (
        layer_output,
        input_gradient,
        attend_total,
        column_totals[0],
        mixer_total,
        vector_totals[0],
        vector_totals[1],
        vector_totals[2],
        widen_total,
        column_totals[1],
        narrow_total,
        vector_totals[3],
        vector_totals[4],
        vector_totals[5],
    )


def solution(mesh):
    return jax.shard_map(
        per_device,
        mesh=mesh,
        in_specs=(
            P(("dp", "col"), "row"),
            P("dp"),
            P("row", "col"),
            P("col", None),
            P("col", "row"),
            P("row"),
            P("row"),
            P("row"),
            P("row", "col"),
            P("col"),
            P("col", "row"),
            P("row"),
            P("row"),
            P("row"),
            P(("dp", "col"), "row"),
        ),
        out_specs=(
            P(("dp", "col"), "row"),
            P(("dp", "col"), "row"),
            P("row", "col"),
            P("col", None),
            P("col", "row"),
            P("row"),
            P("row"),
            P("row"),
            P("row", "col"),
            P("col"),
            P("col", "row"),
            P("row"),
            P("row"),
            P("row"),
        ),
        check_vma=False,
    )
```

```python
import functools

import jax
import jax.numpy as jnp
from jax import lax
from jax.experimental import pallas as pl
from jax.experimental.pallas import tpu as pltpu
from jax.sharding import PartitionSpec as P

D = 1024
HD = 64


EPSILON = 1e-12
MASKED = -1e30


def product(left_side, right_side):
    return jnp.dot(left_side, right_side, preferred_element_type=jnp.float32)


def inner_rows(left_side, right_side):
    return lax.dot_general(
        left_side, right_side, (((0,), (0,)), ((), ())), preferred_element_type=jnp.float32
    )


def outer_back(left_side, right_side):
    return lax.dot_general(
        left_side, right_side, (((1,), (1,)), ((), ())), preferred_element_type=jnp.float32
    )


def gelu_exact(values):
    return jax.nn.gelu(values, approximate=False)


VMEM_BYTES = 48 * 1024 * 1024
MESH = pl.DeviceIdType.MESH


def reduce_levels(dp_count):
    levels = [("dp", 1), ("row", 1)]
    bit = 2
    while bit < dp_count:
        levels.append(("dp", bit))
        bit *= 2
    return levels


def greet(me, count, levels, whole_chain):
    barrier = pltpu.get_barrier_semaphore()
    for axis, bit in levels:
        pl.semaphore_signal(
            barrier, inc=1, device_id={axis: lax.axis_index(axis) ^ bit}, device_id_type=MESH
        )
    if whole_chain:
        for step in range(1, count):
            pl.semaphore_signal(
                barrier, inc=1, device_id={"col": lax.rem(me + step, count)}, device_id_type=MESH
            )
        pl.semaphore_wait(barrier, len(levels) + count - 1)
        return

    @pl.when(me > 0)
    def _():
        pl.semaphore_signal(barrier, inc=1, device_id={"col": me - 1}, device_id_type=MESH)

    @pl.when(me < count - 1)
    def _():
        pl.semaphore_signal(barrier, inc=1, device_id={"col": me + 1}, device_id_type=MESH)

    inner = (me > 0) & (me < count - 1)

    @pl.when(inner)
    def _():
        pl.semaphore_wait(barrier, len(levels) + 2)

    @pl.when(jnp.logical_not(inner))
    def _():
        pl.semaphore_wait(barrier, len(levels) + 1)


def gather_stages(count, block_ref, out_ref, send_sem, recv_sem):
    me = lax.axis_index("col")
    rows = block_ref.shape[0]

    def span(owner):
        return out_ref.at[pl.ds(pl.multiple_of(owner * rows, rows), rows)]

    def hop(source, owner, target, way, step):
        return pltpu.make_async_remote_copy(
            src_ref=source,
            dst_ref=span(owner),
            send_sem=send_sem.at[way, step],
            recv_sem=recv_sem.at[way, step],
            device_id={"col": target},
            device_id_type=MESH,
        )

    def start(step):
        @pl.when((me < count - 1) & (me - step >= 0))
        def _():
            source = block_ref if step == 0 else span(me - step)
            hop(source, me - step, me + 1, 0, step).start()

        @pl.when((me > 0) & (me + step <= count - 1))
        def _():
            source = block_ref if step == 0 else span(me + step)
            hop(source, me + step, me - 1, 1, step).start()

        if step == 0:
            out_ref[pl.ds(pl.multiple_of(me * rows, rows), rows), :] = block_ref[...]

    def arrive(step):
        @pl.when(me - step - 1 >= 0)
        def _():
            hop(span(me - step - 1), me - step - 1, me, 0, step).wait_recv()

        @pl.when(me + step + 1 <= count - 1)
        def _():
            hop(span(me + step + 1), me + step + 1, me, 1, step).wait_recv()

    def middle(step):
        arrive(step - 1)
        start(step)

    def last():
        arrive(count - 2)
        for step in range(count - 1):

            @pl.when((me < count - 1) & (me - step >= 0))
            def _():
                hop(span(me - step), me - step, me + 1, 0, step).wait_send()

            @pl.when((me > 0) & (me + step <= count - 1))
            def _():
                hop(span(me + step), me + step, me - 1, 1, step).wait_send()

    return (
        [functools.partial(start, 0)]
        + [functools.partial(middle, step) for step in range(1, count - 1)]
        + [last]
    )


def scatter_stages(count, part_ref, out_ref, held, sent, send_sem, recv_sem):
    me = lax.axis_index("col")
    rows = out_ref.shape[0]

    def mine(owner):
        return part_ref[pl.ds(pl.multiple_of(owner * rows, rows), rows), :].astype(jnp.float32)

    def hop(way, owner, target):
        return pltpu.make_async_remote_copy(
            src_ref=sent.at[way, owner],
            dst_ref=held.at[way, owner],
            send_sem=send_sem.at[way, owner],
            recv_sem=recv_sem.at[way, owner],
            device_id={"col": target},
            device_id_type=MESH,
        )

    def flows(step):
        return (
            (0, count - 1 - step, me < count - 1 - step),
            (1, step, me > step),
        )

    def move(step):
        for way, owner, inside in flows(step):
            first = me == 0 if way == 0 else me == count - 1
            target = me + 1 if way == 0 else me - 1

            @pl.when(inside & first)
            def _():
                sent[way, owner] = mine(owner).astype(sent.dtype)
                hop(way, owner, target).start()

            @pl.when(inside & jnp.logical_not(first))
            def _():
                hop(way, owner, target).wait_recv()
                total = mine(owner) + held[way, owner].astype(jnp.float32)
                sent[way, owner] = total.astype(sent.dtype)
                hop(way, owner, target).start()

    def last():
        out_ref[...] = mine(me)

        @pl.when(me > 0)
        def _():
            hop(0, me, me).wait_recv()
            out_ref[...] += held[0, me].astype(jnp.float32)

        @pl.when(me < count - 1)
        def _():
            hop(1, me, me).wait_recv()
            out_ref[...] += held[1, me].astype(jnp.float32)

        for step in range(count - 1):
            for way, owner, inside in flows(step):

                @pl.when(inside)
                def _():
                    hop(way, owner, me).wait_send()

    return [functools.partial(move, step) for step in range(count - 1)] + [last]


def weight_shape(part_shape, split):
    rows, width = part_shape
    return (rows // 2, width) if split == 0 else (rows, width // 2)


def weight_scratch(part_shape, split, dp_count):
    rows, width = weight_shape(part_shape, split)
    count = len(reduce_levels(dp_count))
    half = rows // 2
    scratch = [
        pltpu.VMEM((2, half, width), jnp.bfloat16),
        pltpu.VMEM((half, width), jnp.bfloat16),
        pltpu.VMEM((half, width), jnp.bfloat16),
        pltpu.VMEM((half, width), jnp.float32),
        pltpu.VMEM((rows, width), jnp.bfloat16),
        pltpu.SemaphoreType.DMA((2 * count + 1,)),
        pltpu.SemaphoreType.DMA((2 * count + 1,)),
    ]
    for level in range(2, count):
        piece = half >> (level - 1)
        scratch += [pltpu.VMEM((piece, width), jnp.bfloat16)] * 2
    return scratch


def weight_stages(split, dp_count, part_ref, out_ref, scratch):
    near, toward, beside, total, whole, send_sem, recv_sem = scratch[:7]
    deeper = scratch[7:]
    levels = reduce_levels(dp_count)
    rows, width = out_ref.shape
    half = rows // 2
    dp, row = lax.axis_index("dp"), lax.axis_index("row")

    def at(side, start, size):
        if split == 0:
            return (pl.ds(pl.multiple_of(side * rows + start, size), size), slice(None))
        return (
            pl.ds(pl.multiple_of(start, size), size),
            pl.ds(pl.multiple_of(side * width, width), width),
        )

    def copy(source, landing, place, level):
        axis, bit = levels[level]
        return pltpu.make_async_remote_copy(
            src_ref=source,
            dst_ref=landing,
            send_sem=send_sem.at[place],
            recv_sem=recv_sem.at[place],
            device_id={axis: lax.axis_index(axis) ^ bit},
            device_id_type=MESH,
        )

    low = dp % 2
    core_copies = [
        copy(part_ref.at[at(side, (1 - low) * half, half)], near.at[place], place, 0)
        for place, side in ((0, 1 - row), (1, row))
    ]
    row_copy = copy(toward, beside, 2, 1)
    waits = core_copies + [row_copy]
    stages = []

    def begin():
        for item in core_copies:
            item.start()

    def summed(side, place):
        return part_ref[at(side, low * half, half)].astype(jnp.float32) + near[place].astype(
            jnp.float32
        )

    def core_done():
        core_copies[0].wait_recv()
        toward[...] = summed(1 - row, 0).astype(jnp.bfloat16)
        row_copy.start()
        core_copies[1].wait_recv()
        total[...] = summed(row, 1)

    kept, size = 0, half
    halvings = []
    for level in range(2, len(levels)):
        side = (dp // levels[level][1]) % 2
        size //= 2
        item = copy(deeper[2 * level - 4], deeper[2 * level - 3], level + 1, level)
        waits.append(item)
        halvings.append((level, item, kept + (1 - side) * size, kept + side * size, size))
        kept = kept + side * size

    def send_halving(entry):
        level, item, other, _, extent = entry
        deeper[2 * level - 4][...] = total[
            pl.ds(pl.multiple_of(other, extent), extent), :
        ].astype(jnp.bfloat16)
        item.start()

    def take_halving(entry):
        level, item, _, own, extent = entry
        item.wait_recv()
        place = pl.ds(pl.multiple_of(own, extent), extent)
        total[place, :] = total[place, :] + deeper[2 * level - 3][...].astype(jnp.float32)

    doublings = []
    start, extent = low * half + kept, size
    for level in list(range(len(levels) - 1, 1, -1)) + [0]:
        place = len(levels) + 1 + len(doublings)
        ref = whole.at[pl.ds(pl.multiple_of(start, extent), extent)]
        side = (dp // levels[level][1]) % 2
        item = copy(ref, ref, place, level)
        other = whole.at[
            pl.ds(pl.multiple_of(start + (1 - 2 * side) * extent, extent), extent)
        ]
        doublings.append((item, copy(other, other, place, level)))
        start, extent = start - side * extent, 2 * extent

    def start_doubling():
        own = pl.ds(pl.multiple_of(low * half + kept, size), size)
        whole[own, :] = total[pl.ds(pl.multiple_of(kept, size), size), :].astype(jnp.bfloat16)
        doublings[0][0].start()

    def row_done():
        row_copy.wait_recv()
        total[...] += beside[...].astype(jnp.float32)
        if halvings:
            send_halving(halvings[0])
        else:
            start_doubling()

    def halved(position):
        take_halving(halvings[position])
        if position + 1 < len(halvings):
            send_halving(halvings[position + 1])
        else:
            start_doubling()

    def doubled(position):
        doublings[position][1].wait_recv()
        if position + 1 < len(doublings):
            doublings[position + 1][0].start()
        else:
            out_ref[...] = whole[...].astype(jnp.float32)
            for item in waits:
                item.wait_send()
            for item, _ in doublings:
                item.wait_send()

    stages = [begin, core_done, row_done]
    stages += [functools.partial(halved, position) for position in range(len(halvings))]
    stages += [functools.partial(doubled, position) for position in range(len(doublings))]
    return stages


def vector_stages(count, dp_count, shared, part_ref, out_ref, totals, landed, across, send_sem, recv_sem):
    levels = reduce_levels(dp_count)
    me = lax.axis_index("col")

    def copy(level):
        axis, bit = levels[level]
        return pltpu.make_async_remote_copy(
            src_ref=part_ref if level == 0 else totals.at[level - 1],
            dst_ref=landed.at[level],
            send_sem=send_sem.at[level],
            recv_sem=recv_sem.at[level],
            device_id={axis: lax.axis_index(axis) ^ bit},
            device_id_type=MESH,
        )

    def spread(step):
        return pltpu.make_async_remote_copy(
            src_ref=totals.at[len(levels) - 1],
            dst_ref=across.at[me],
            send_sem=send_sem.at[len(levels) + step],
            recv_sem=recv_sem.at[len(levels) + step],
            device_id={"col": lax.rem(me + step, count)},
            device_id_type=MESH,
        )

    def arrival(step):
        return pltpu.make_async_remote_copy(
            src_ref=totals.at[len(levels) - 1],
            dst_ref=across.at[lax.rem(me - step + count, count)],
            send_sem=send_sem.at[len(levels) + step],
            recv_sem=recv_sem.at[len(levels) + step],
            device_id={"col": lax.rem(me + step, count)},
            device_id_type=MESH,
        )

    def take(level):
        copy(level).wait_recv()
        held = part_ref[...] if level == 0 else totals[level - 1]
        totals[level] = held + landed[level]
        if level + 1 < len(levels):
            copy(level + 1).start()
        else:
            across[me] = totals[level]
            for step in range(1, count):
                spread(step).start()

    def finish():
        for step in range(1, count):
            arrival(step).wait_recv()
        whole = across[0]
        for other in range(1, count):
            whole = whole + across[other]
        shared_rows = lax.broadcasted_iota(jnp.int32, whole.shape, 0) < shared
        out_ref[...] = jnp.where(shared_rows, whole, totals[len(levels) - 1])
        for level in range(len(levels)):
            copy(level).wait_send()
        for step in range(1, count):
            spread(step).wait_send()

    return (
        [lambda: copy(0).start()]
        + [functools.partial(take, level) for level in range(len(levels))]
        + [finish]
    )


def chain_kernel(kind, split, shared, count, dp_count, sizes, *refs):
    me = lax.axis_index("col")
    refs = list(refs)

    def pull(number):
        taken = refs[:number]
        del refs[:number]
        return taken

    extras = (split is not None) + (shared > 0)
    inputs, outputs = pull(1 + extras), pull(1 + extras)
    greet(me, count, reduce_levels(dp_count) if extras else [], shared > 0)
    chain = (gather_stages if kind == "gather" else scatter_stages)(
        count, inputs[0], outputs[0], *pull(sizes[0])
    )
    weight, vector = [], []
    if split is not None:
        weight = weight_stages(split, dp_count, inputs[1], outputs[1], pull(sizes[1]))
    if shared > 0:
        vector = vector_stages(count, dp_count, shared, inputs[2], outputs[2], *pull(sizes[2]))
    order = []
    for position in range(max(len(chain), len(weight), len(vector))):
        if position < len(chain):
            order.append(chain[position])
        if position < len(vector):
            order.append(vector[position])
        if position < len(weight):
            order.append(weight[position])
    for stage in order:
        stage()


def chain_call(kind, ident, block, weight=None, split=None, vectors=None, shared=0):
    count, dp_count = lax.axis_size("col"), lax.axis_size("dp")
    rows, width = block.shape
    operands, sizes = [block], [0, 0, 0]
    if kind == "gather":
        shapes = [jax.ShapeDtypeStruct((count * rows, width), block.dtype)]
        scratch = [pltpu.SemaphoreType.DMA((2, count - 1))] * 2
    else:
        rows //= count
        shapes = [jax.ShapeDtypeStruct((rows, width), jnp.float32)]
        scratch = [pltpu.VMEM((2, count, rows, width), jnp.bfloat16)] * 2
        scratch += [pltpu.SemaphoreType.DMA((2, count))] * 2
    sizes[0] = len(scratch)
    if weight is not None:
        operands.append(weight)
        shapes.append(jax.ShapeDtypeStruct(weight_shape(weight.shape, split), jnp.float32))
        more = weight_scratch(weight.shape, split, dp_count)
        sizes[1] = len(more)
        scratch += more
    if vectors is not None:
        operands.append(vectors)
        shapes.append(jax.ShapeDtypeStruct(vectors.shape, vectors.dtype))
        levels = len(reduce_levels(dp_count))
        more = [
            pltpu.VMEM((levels,) + vectors.shape, vectors.dtype),
            pltpu.VMEM((levels,) + vectors.shape, vectors.dtype),
            pltpu.VMEM((count,) + vectors.shape, vectors.dtype),
            pltpu.SemaphoreType.DMA((levels + count,)),
            pltpu.SemaphoreType.DMA((levels + count,)),
        ]
        sizes[2] = len(more)
        scratch += more
    results = pl.pallas_call(
        functools.partial(chain_kernel, kind, split, shared, count, dp_count, tuple(sizes)),
        out_shape=shapes,
        in_specs=[pl.BlockSpec(memory_space=pltpu.VMEM)] * len(operands),
        out_specs=[pl.BlockSpec(memory_space=pltpu.VMEM)] * len(operands),
        scratch_shapes=scratch,
        compiler_params=pltpu.CompilerParams(
            collective_id=ident, has_side_effects=True, vmem_limit_bytes=VMEM_BYTES
        ),
        cost_estimate=pl.CostEstimate(
            flops=0, bytes_accessed=60 * 1024 * 1024, transcendentals=0
        ),
        name="chain_" + kind + str(ident),
    )(*operands)
    return results[0] if len(results) == 1 else results


def gather_tokens(block):
    return chain_call("gather", 0, block)


def scatter_tokens(part):
    return chain_call("scatter", 1, part)


def slot_moves(swap):
    col_count = lax.axis_size("col")
    half = col_count // 2
    pairs = []
    for row in range(2):
        for col in range(col_count):
            there = (col // half) * col_count + 2 * (col % half) + (row ^ swap)
            pairs.append((row * col_count + col, there))
    return pairs


def to_slot_rows(stored):
    row, col = lax.axis_index("row"), lax.axis_index("col")
    rows = stored.shape[0] // 2
    landed = []
    for swap in range(2):
        block = lax.dynamic_slice_in_dim(stored, (row ^ swap) * rows, rows, 0)
        landed.append(lax.ppermute(block, ("row", "col"), slot_moves(swap)))
    odd = (col % 2) == 1
    left = jnp.where(odd, landed[1], landed[0])
    right = jnp.where(odd, landed[0], landed[1])
    return jnp.concatenate([left, right], axis=1)


def from_slot_rows(block):
    row, col = lax.axis_index("row"), lax.axis_index("col")
    width = block.shape[1] // 2
    landed = []
    for swap in range(2):
        piece = lax.dynamic_slice_in_dim(block, ((col % 2) ^ swap) * width, width, 1)
        pairs = [(there, here) for here, there in slot_moves(swap)]
        landed.append(lax.ppermute(piece, ("row", "col"), pairs))
    upper = jnp.where(row == 1, landed[1], landed[0])
    lower = jnp.where(row == 1, landed[0], landed[1])
    return jnp.concatenate([upper, lower], axis=0)


def norm_forward(summed, gain_row, shift_row):
    average = jnp.mean(summed, axis=1, keepdims=True)
    centred = summed - average
    variance = jnp.mean(centred * centred, axis=1, keepdims=True)
    inverse = lax.rsqrt(variance + EPSILON)
    normal = centred * inverse
    return (normal * gain_row + shift_row, normal, inverse)


def norm_backward(upstream, normal, inverse, gain_row):
    scaled = upstream * gain_row
    average = jnp.mean(scaled, axis=1, keepdims=True)
    crossed = jnp.mean(scaled * normal, axis=1, keepdims=True)
    return (scaled - average - normal * crossed) * inverse


def slot_scores(query_part, key_part, length):
    scores = jnp.einsum(
        "qhd,khd->hqk", query_part, key_part, preferred_element_type=jnp.float32
    ) * HD ** (-0.5)
    valid_keys = lax.iota(jnp.int32, key_part.shape[0]) < length
    return jnp.where(valid_keys[None, None, :], scores, MASKED)


def slot_forward(slot_item):
    query_part, key_part, value_part, length = slot_item
    scores = slot_scores(query_part, key_part, length)
    row_top = jnp.max(scores, axis=2, keepdims=True)
    exponent = jnp.exp(scores - row_top)
    row_total = jnp.sum(exponent, axis=2, keepdims=True)
    probabilities = (exponent / row_total).astype(jnp.bfloat16)
    mixed = jnp.einsum(
        "hqk,khd->qhd", probabilities, value_part, preferred_element_type=jnp.float32
    )
    return (mixed.astype(jnp.bfloat16), (row_top + jnp.log(row_total))[:, :, 0])


def slot_backward(slot_item):
    query_part, key_part, value_part, length, logsum, grad_heads = slot_item
    probabilities = jnp.exp(slot_scores(query_part, key_part, length) - logsum[:, :, None])
    grad_probs = jnp.einsum(
        "qhd,khd->hqk", grad_heads, value_part, preferred_element_type=jnp.float32
    )
    grad_values = jnp.einsum(
        "hqk,qhd->khd",
        probabilities.astype(jnp.bfloat16),
        grad_heads,
        preferred_element_type=jnp.float32,
    )
    along = jnp.sum(probabilities * grad_probs, axis=2, keepdims=True)
    grad_scores = (probabilities * (grad_probs - along)).astype(jnp.bfloat16)
    grad_query = jnp.einsum(
        "hqk,khd->qhd", grad_scores, key_part, preferred_element_type=jnp.float32
    ) * HD ** (-0.5)
    grad_keys = jnp.einsum(
        "hqk,qhd->khd", grad_scores, query_part, preferred_element_type=jnp.float32
    ) * HD ** (-0.5)
    return jnp.stack([grad_query, grad_keys, grad_values], axis=2)


def weight_total(part, dimension):
    part = lax.psum_scatter(
        part.astype(jnp.bfloat16), "row", scatter_dimension=dimension, tiled=True
    )
    return lax.psum(part, "dp").astype(jnp.float32)


def per_device(
    layer_input,
    lengths,
    attend_weight,
    attend_bias,
    mixer_weight,
    mixer_bias,
    first_gain,
    first_shift,
    widen_weight,
    widen_bias,
    narrow_weight,
    narrow_bias,
    second_gain,
    second_shift,
    cotangent,
):
    row_rank = lax.axis_index("row")
    col_rank = lax.axis_index("col")
    heads_here = attend_bias.shape[0]
    input_block = to_slot_rows(layer_input)
    block_rows = input_block.shape[0]
    length = lax.dynamic_index_in_dim(lengths, row_rank, 0, keepdims=False)
    vectors = jnp.stack(
        [mixer_bias, first_gain, first_shift, narrow_bias, second_gain, second_shift]
    )
    vectors = lax.all_gather(vectors, "row", axis=1, tiled=True)
    mixer_bias, first_gain, first_shift, narrow_bias, second_gain, second_shift = vectors
    attend_weight = lax.all_gather(attend_weight, "row", axis=0, tiled=True)
    mixer_weight = lax.all_gather(mixer_weight, "row", axis=1, tiled=True)
    widen_weight = lax.all_gather(widen_weight, "row", axis=0, tiled=True)
    narrow_weight = lax.all_gather(narrow_weight, "row", axis=1, tiled=True)

    gathered_input = gather_tokens(input_block)
    slot_rows = gathered_input.shape[0]
    bias_full = jnp.concatenate(
        [attend_bias[:, :HD], jnp.zeros((heads_here, HD), jnp.float32), attend_bias[:, HD:]],
        axis=1,
    ).reshape(heads_here * 3 * HD)
    packed = (product(gathered_input, attend_weight) + bias_full).astype(jnp.bfloat16)
    split_heads = packed.reshape(slot_rows, heads_here, 3, HD)
    query_all = split_heads[:, :, 0]
    keys_all = split_heads[:, :, 1]
    values_all = split_heads[:, :, 2]
    mixed, logsum = slot_forward((query_all, keys_all, values_all, length))
    mixed_block = mixed.reshape(slot_rows, heads_here * HD)
    attended = scatter_tokens(product(mixed_block, mixer_weight)) + mixer_bias
    first_out, first_normal, first_inverse = norm_forward(
        input_block.astype(jnp.float32) + attended, first_gain, first_shift
    )
    gathered_first = gather_tokens(first_out.astype(jnp.bfloat16))
    widened = product(gathered_first, widen_weight) + widen_bias
    active, gelu_pull = jax.vjp(gelu_exact, widened)
    active_block = active.astype(jnp.bfloat16)
    narrowed = scatter_tokens(product(active_block, narrow_weight)) + narrow_bias
    second_out, second_normal, second_inverse = norm_forward(
        first_out + narrowed, second_gain, second_shift
    )
    layer_output = from_slot_rows(second_out.astype(jnp.bfloat16))
    positions = col_rank * block_rows + lax.iota(jnp.int32, block_rows)
    upstream = jnp.where(
        (positions < length)[:, None], to_slot_rows(cotangent).astype(jnp.float32), 0.0
    )
    second_gain_part = jnp.sum(upstream * second_normal, axis=0)
    second_shift_part = jnp.sum(upstream, axis=0)
    grad_second = norm_backward(upstream, second_normal, second_inverse, second_gain)
    grad_narrowed = grad_second.astype(jnp.bfloat16)
    narrow_bias_part = jnp.sum(grad_narrowed, axis=0, dtype=jnp.float32)
    grad_narrow_block = gather_tokens(grad_narrowed)
    narrow_part = inner_rows(active_block, grad_narrow_block).astype(jnp.bfloat16)
    grad_active = outer_back(grad_narrow_block, narrow_weight)
    grad_widened = gelu_pull(grad_active)[0].astype(jnp.bfloat16)
    widen_bias_part = jnp.sum(grad_widened, axis=0, dtype=jnp.float32)
    grad_first, narrow_total = chain_call(
        "scatter", 2, outer_back(grad_widened, widen_weight), narrow_part, 1
    )
    grad_first = grad_first + grad_second
    widen_part = inner_rows(gathered_first, grad_widened).astype(jnp.bfloat16)
    first_gain_part = jnp.sum(grad_first * first_normal, axis=0)
    first_shift_part = jnp.sum(grad_first, axis=0)
    grad_attended = norm_backward(grad_first, first_normal, first_inverse, first_gain)
    grad_mix = grad_attended.astype(jnp.bfloat16)
    mixer_bias_part = jnp.sum(grad_mix, axis=0, dtype=jnp.float32)
    grad_mixer_block, widen_total = chain_call("gather", 3, grad_mix, widen_part, 0)
    mixer_total = weight_total(inner_rows(mixed_block, grad_mixer_block), 1)
    grad_mixed = outer_back(grad_mixer_block, mixer_weight).astype(jnp.bfloat16)
    grad_heads = grad_mixed.reshape(slot_rows, heads_here, HD)
    grad_slots = slot_backward((query_all, keys_all, values_all, length, logsum, grad_heads))
    grad_packed = grad_slots.reshape(slot_rows, heads_here * 3 * HD).astype(jnp.bfloat16)
    packed_sums = jnp.sum(grad_packed, axis=0, dtype=jnp.float32).reshape(heads_here, 3, HD)
    attend_bias_part = jnp.concatenate([packed_sums[:, 0], packed_sums[:, 2]], axis=1)
    attend_part = inner_rows(gathered_input, grad_packed).astype(jnp.bfloat16)
    model = mixer_bias_part.shape[0]
    attend_bias_flat = attend_bias_part.reshape(-1)
    vector_parts = jnp.stack(
        [
            mixer_bias_part,
            first_gain_part,
            first_shift_part,
            narrow_bias_part,
            second_gain_part,
            second_shift_part,
            jnp.pad(widen_bias_part, (0, model - widen_bias_part.shape[0])),
            jnp.pad(attend_bias_flat, (0, model - attend_bias_flat.shape[0])),
        ]
    )
    input_gradient, attend_total, vector_sums = chain_call(
        "scatter", 4, outer_back(grad_packed, attend_weight), attend_part, 0, vector_parts, 6
    )
    input_gradient = from_slot_rows(input_gradient + grad_attended)
    half = model // 2
    vector_totals = lax.dynamic_slice_in_dim(vector_sums, row_rank * half, half, 1)
    column_totals = (
        vector_sums[7, : attend_bias_flat.shape[0]].reshape(attend_bias_part.shape),
        vector_sums[6, : widen_bias_part.shape[0]],
    )
    return (
        layer_output,
        input_gradient,
        attend_total,
        column_totals[0],
        mixer_total,
        vector_totals[0],
        vector_totals[1],
        vector_totals[2],
        widen_total,
        column_totals[1],
        narrow_total,
        vector_totals[3],
        vector_totals[4],
        vector_totals[5],
    )


def solution(mesh):
    return jax.shard_map(
        per_device,
        mesh=mesh,
        in_specs=(
            P(("dp", "col"), "row"),
            P("dp"),
            P("row", "col"),
            P("col", None),
            P("col", "row"),
            P("row"),
            P("row"),
            P("row"),
            P("row", "col"),
            P("col"),
            P("col", "row"),
            P("row"),
            P("row"),
            P("row"),
            P(("dp", "col"), "row"),
        ),
        out_specs=(
            P(("dp", "col"), "row"),
            P(("dp", "col"), "row"),
            P("row", "col"),
            P("col", None),
            P("col", "row"),
            P("row"),
            P("row"),
            P("row"),
            P("row", "col"),
            P("col"),
            P("col", "row"),
            P("row"),
            P("row"),
            P("row"),
        ),
        check_vma=False,
    )
```

```python
import functools

import jax
import jax.numpy as jnp
from jax import lax
from jax.experimental import pallas as pl
from jax.experimental.pallas import tpu as pltpu
from jax.sharding import PartitionSpec as P

D = 1024
HD = 64


EPSILON = 1e-12
MASKED = -1e30


def product(left_side, right_side):
    return jnp.dot(left_side, right_side, preferred_element_type=jnp.float32)


def inner_rows(left_side, right_side):
    return lax.dot_general(
        left_side, right_side, (((0,), (0,)), ((), ())), preferred_element_type=jnp.float32
    )


def outer_back(left_side, right_side):
    return lax.dot_general(
        left_side, right_side, (((1,), (1,)), ((), ())), preferred_element_type=jnp.float32
    )


def gelu_exact(values):
    return jax.nn.gelu(values, approximate=False)


VMEM_BYTES = 48 * 1024 * 1024
MESH = pl.DeviceIdType.MESH
CHUNKS = 2


def reduce_levels(dp_count):
    levels = [("dp", 1), ("row", 1)]
    bit = 2
    while bit < dp_count:
        levels.append(("dp", bit))
        bit *= 2
    return levels


def greet(me, count, levels, whole_chain):
    barrier = pltpu.get_barrier_semaphore()
    for axis, bit in levels:
        pl.semaphore_signal(
            barrier, inc=1, device_id={axis: lax.axis_index(axis) ^ bit}, device_id_type=MESH
        )
    if whole_chain:
        for step in range(1, count):
            pl.semaphore_signal(
                barrier, inc=1, device_id={"col": lax.rem(me + step, count)}, device_id_type=MESH
            )
        pl.semaphore_wait(barrier, len(levels) + count - 1)
        return

    @pl.when(me > 0)
    def _():
        pl.semaphore_signal(barrier, inc=1, device_id={"col": me - 1}, device_id_type=MESH)

    @pl.when(me < count - 1)
    def _():
        pl.semaphore_signal(barrier, inc=1, device_id={"col": me + 1}, device_id_type=MESH)

    inner = (me > 0) & (me < count - 1)

    @pl.when(inner)
    def _():
        pl.semaphore_wait(barrier, len(levels) + 2)

    @pl.when(jnp.logical_not(inner))
    def _():
        pl.semaphore_wait(barrier, len(levels) + 1)


def gather_stages(count, block_ref, out_ref, send_sem, recv_sem):
    me = lax.axis_index("col")
    rows = block_ref.shape[0]

    def span(owner):
        return out_ref.at[pl.ds(pl.multiple_of(owner * rows, rows), rows)]

    def hop(source, owner, target, way, step):
        return pltpu.make_async_remote_copy(
            src_ref=source,
            dst_ref=span(owner),
            send_sem=send_sem.at[way, step],
            recv_sem=recv_sem.at[way, step],
            device_id={"col": target},
            device_id_type=MESH,
        )

    def start(step):
        @pl.when((me < count - 1) & (me - step >= 0))
        def _():
            source = block_ref if step == 0 else span(me - step)
            hop(source, me - step, me + 1, 0, step).start()

        @pl.when((me > 0) & (me + step <= count - 1))
        def _():
            source = block_ref if step == 0 else span(me + step)
            hop(source, me + step, me - 1, 1, step).start()

        if step == 0:
            out_ref[pl.ds(pl.multiple_of(me * rows, rows), rows), :] = block_ref[...]

    def arrive(step):
        @pl.when(me - step - 1 >= 0)
        def _():
            hop(span(me - step - 1), me - step - 1, me, 0, step).wait_recv()

        @pl.when(me + step + 1 <= count - 1)
        def _():
            hop(span(me + step + 1), me + step + 1, me, 1, step).wait_recv()

    def middle(step):
        arrive(step - 1)
        start(step)

    def last():
        arrive(count - 2)
        for step in range(count - 1):

            @pl.when((me < count - 1) & (me - step >= 0))
            def _():
                hop(span(me - step), me - step, me + 1, 0, step).wait_send()

            @pl.when((me > 0) & (me + step <= count - 1))
            def _():
                hop(span(me + step), me + step, me - 1, 1, step).wait_send()

    return (
        [functools.partial(start, 0)]
        + [functools.partial(middle, step) for step in range(1, count - 1)]
        + [last]
    )


def scatter_stages(count, part_ref, out_ref, held, sent, send_sem, recv_sem):
    me = lax.axis_index("col")
    rows = out_ref.shape[0] // CHUNKS

    def mine(owner, chunk):
        start = pl.multiple_of((owner * CHUNKS + chunk) * rows, rows)
        return part_ref[pl.ds(start, rows), :].astype(jnp.float32)

    def hop(way, owner, chunk, target):
        return pltpu.make_async_remote_copy(
            src_ref=sent.at[way, owner, chunk],
            dst_ref=held.at[way, owner, chunk],
            send_sem=send_sem.at[way, owner, chunk],
            recv_sem=recv_sem.at[way, owner, chunk],
            device_id={"col": target},
            device_id_type=MESH,
        )

    def flows(step):
        return (
            (0, count - 1 - step, me < count - 1 - step),
            (1, step, me > step),
        )

    def one(way, owner, inside, chunk):
        first = me == 0 if way == 0 else me == count - 1
        target = me + 1 if way == 0 else me - 1

        @pl.when(inside & first)
        def _():
            sent[way, owner, chunk] = mine(owner, chunk).astype(sent.dtype)
            hop(way, owner, chunk, target).start()

        @pl.when(inside & jnp.logical_not(first))
        def _():
            hop(way, owner, chunk, target).wait_recv()
            total = mine(owner, chunk) + held[way, owner, chunk].astype(jnp.float32)
            sent[way, owner, chunk] = total.astype(sent.dtype)
            hop(way, owner, chunk, target).start()

    def move(step):
        for chunk in range(CHUNKS):
            for way, owner, inside in flows(step):
                one(way, owner, inside, chunk)

    def last():
        for chunk in range(CHUNKS):
            place = pl.ds(chunk * rows, rows)
            out_ref[place, :] = mine(me, chunk)

            @pl.when(me > 0)
            def _():
                hop(0, me, chunk, me).wait_recv()
                out_ref[place, :] += held[0, me, chunk].astype(jnp.float32)

            @pl.when(me < count - 1)
            def _():
                hop(1, me, chunk, me).wait_recv()
                out_ref[place, :] += held[1, me, chunk].astype(jnp.float32)

        for step in range(count - 1):
            for way, owner, inside in flows(step):

                @pl.when(inside)
                def _():
                    for chunk in range(CHUNKS):
                        hop(way, owner, chunk, me).wait_send()

    return [functools.partial(move, step) for step in range(count - 1)] + [last]


def weight_shape(part_shape, split):
    rows, width = part_shape
    return (rows // 2, width) if split == 0 else (rows, width // 2)


def weight_scratch(part_shape, split, dp_count):
    rows, width = weight_shape(part_shape, split)
    count = len(reduce_levels(dp_count))
    half = rows // 2
    scratch = [
        pltpu.VMEM((2, half, width), jnp.bfloat16),
        pltpu.VMEM((half, width), jnp.bfloat16),
        pltpu.VMEM((half, width), jnp.bfloat16),
        pltpu.VMEM((half, width), jnp.float32),
        pltpu.VMEM((rows, width), jnp.bfloat16),
        pltpu.SemaphoreType.DMA((2 * count + 1,)),
        pltpu.SemaphoreType.DMA((2 * count + 1,)),
    ]
    for level in range(2, count):
        piece = half >> (level - 1)
        scratch += [pltpu.VMEM((piece, width), jnp.bfloat16)] * 2
    return scratch


def weight_stages(split, dp_count, part_ref, out_ref, scratch):
    near, toward, beside, total, whole, send_sem, recv_sem = scratch[:7]
    deeper = scratch[7:]
    levels = reduce_levels(dp_count)
    rows, width = out_ref.shape
    half = rows // 2
    dp, row = lax.axis_index("dp"), lax.axis_index("row")

    def at(side, start, size):
        if split == 0:
            return (pl.ds(pl.multiple_of(side * rows + start, size), size), slice(None))
        return (
            pl.ds(pl.multiple_of(start, size), size),
            pl.ds(pl.multiple_of(side * width, width), width),
        )

    def copy(source, landing, place, level):
        axis, bit = levels[level]
        return pltpu.make_async_remote_copy(
            src_ref=source,
            dst_ref=landing,
            send_sem=send_sem.at[place],
            recv_sem=recv_sem.at[place],
            device_id={axis: lax.axis_index(axis) ^ bit},
            device_id_type=MESH,
        )

    low = dp % 2
    core_copies = [
        copy(part_ref.at[at(side, (1 - low) * half, half)], near.at[place], place, 0)
        for place, side in ((0, 1 - row), (1, row))
    ]
    row_copy = copy(toward, beside, 2, 1)
    waits = core_copies + [row_copy]
    stages = []

    def begin():
        for item in core_copies:
            item.start()

    def summed(side, place):
        return part_ref[at(side, low * half, half)].astype(jnp.float32) + near[place].astype(
            jnp.float32
        )

    def core_done():
        core_copies[0].wait_recv()
        toward[...] = summed(1 - row, 0).astype(jnp.bfloat16)
        row_copy.start()
        core_copies[1].wait_recv()
        total[...] = summed(row, 1)

    kept, size = 0, half
    halvings = []
    for level in range(2, len(levels)):
        side = (dp // levels[level][1]) % 2
        size //= 2
        item = copy(deeper[2 * level - 4], deeper[2 * level - 3], level + 1, level)
        waits.append(item)
        halvings.append((level, item, kept + (1 - side) * size, kept + side * size, size))
        kept = kept + side * size

    def send_halving(entry):
        level, item, other, _, extent = entry
        deeper[2 * level - 4][...] = total[
            pl.ds(pl.multiple_of(other, extent), extent), :
        ].astype(jnp.bfloat16)
        item.start()

    def take_halving(entry):
        level, item, _, own, extent = entry
        item.wait_recv()
        place = pl.ds(pl.multiple_of(own, extent), extent)
        total[place, :] = total[place, :] + deeper[2 * level - 3][...].astype(jnp.float32)

    doublings = []
    start, extent = low * half + kept, size
    for level in list(range(len(levels) - 1, 1, -1)) + [0]:
        place = len(levels) + 1 + len(doublings)
        ref = whole.at[pl.ds(pl.multiple_of(start, extent), extent)]
        side = (dp // levels[level][1]) % 2
        item = copy(ref, ref, place, level)
        other = whole.at[
            pl.ds(pl.multiple_of(start + (1 - 2 * side) * extent, extent), extent)
        ]
        doublings.append((item, copy(other, other, place, level)))
        start, extent = start - side * extent, 2 * extent

    def start_doubling():
        own = pl.ds(pl.multiple_of(low * half + kept, size), size)
        whole[own, :] = total[pl.ds(pl.multiple_of(kept, size), size), :].astype(jnp.bfloat16)
        doublings[0][0].start()

    def row_done():
        row_copy.wait_recv()
        total[...] += beside[...].astype(jnp.float32)
        if halvings:
            send_halving(halvings[0])
        else:
            start_doubling()

    def halved(position):
        take_halving(halvings[position])
        if position + 1 < len(halvings):
            send_halving(halvings[position + 1])
        else:
            start_doubling()

    def doubled(position):
        doublings[position][1].wait_recv()
        if position + 1 < len(doublings):
            doublings[position + 1][0].start()
        else:
            out_ref[...] = whole[...].astype(jnp.float32)
            for item in waits:
                item.wait_send()
            for item, _ in doublings:
                item.wait_send()

    stages = [begin, core_done, row_done]
    stages += [functools.partial(halved, position) for position in range(len(halvings))]
    stages += [functools.partial(doubled, position) for position in range(len(doublings))]
    return stages


def vector_stages(count, dp_count, shared, part_ref, out_ref, totals, landed, across, send_sem, recv_sem):
    levels = reduce_levels(dp_count)
    me = lax.axis_index("col")

    def copy(level):
        axis, bit = levels[level]
        return pltpu.make_async_remote_copy(
            src_ref=part_ref if level == 0 else totals.at[level - 1],
            dst_ref=landed.at[level],
            send_sem=send_sem.at[level],
            recv_sem=recv_sem.at[level],
            device_id={axis: lax.axis_index(axis) ^ bit},
            device_id_type=MESH,
        )

    def spread(step):
        return pltpu.make_async_remote_copy(
            src_ref=totals.at[len(levels) - 1],
            dst_ref=across.at[me],
            send_sem=send_sem.at[len(levels) + step],
            recv_sem=recv_sem.at[len(levels) + step],
            device_id={"col": lax.rem(me + step, count)},
            device_id_type=MESH,
        )

    def arrival(step):
        return pltpu.make_async_remote_copy(
            src_ref=totals.at[len(levels) - 1],
            dst_ref=across.at[lax.rem(me - step + count, count)],
            send_sem=send_sem.at[len(levels) + step],
            recv_sem=recv_sem.at[len(levels) + step],
            device_id={"col": lax.rem(me + step, count)},
            device_id_type=MESH,
        )

    def take(level):
        copy(level).wait_recv()
        held = part_ref[...] if level == 0 else totals[level - 1]
        totals[level] = held + landed[level]
        if level + 1 < len(levels):
            copy(level + 1).start()
        else:
            across[me] = totals[level]
            for step in range(1, count):
                spread(step).start()

    def finish():
        for step in range(1, count):
            arrival(step).wait_recv()
        whole = across[0]
        for other in range(1, count):
            whole = whole + across[other]
        shared_rows = lax.broadcasted_iota(jnp.int32, whole.shape, 0) < shared
        out_ref[...] = jnp.where(shared_rows, whole, totals[len(levels) - 1])
        for level in range(len(levels)):
            copy(level).wait_send()
        for step in range(1, count):
            spread(step).wait_send()

    return (
        [lambda: copy(0).start()]
        + [functools.partial(take, level) for level in range(len(levels))]
        + [finish]
    )


def chain_kernel(kind, splits, shared, count, dp_count, sizes, *refs):
    me = lax.axis_index("col")
    refs = list(refs)

    def pull(number):
        taken = refs[:number]
        del refs[:number]
        return taken

    extras = len(splits) + (shared > 0)
    inputs, outputs = pull(1 + extras), pull(1 + extras)
    greet(me, count, reduce_levels(dp_count) if extras else [], shared > 0)
    lines = [
        (gather_stages if kind == "gather" else scatter_stages)(
            count, inputs[0], outputs[0], *pull(sizes[0])
        )
    ]
    for place, split in enumerate(splits):
        lines.append(
            weight_stages(
                split, dp_count, inputs[1 + place], outputs[1 + place], pull(sizes[1 + place])
            )
        )
    if shared > 0:
        lines.append(
            vector_stages(count, dp_count, shared, inputs[-1], outputs[-1], *pull(sizes[-1]))
        )
    for position in range(max(len(line) for line in lines)):
        for line in lines:
            if position < len(line):
                line[position]()


def chain_call(kind, ident, block, weights=(), splits=(), vectors=None, shared=0):
    count, dp_count = lax.axis_size("col"), lax.axis_size("dp")
    rows, width = block.shape
    operands, sizes = [block], []
    if kind == "gather":
        shapes = [jax.ShapeDtypeStruct((count * rows, width), block.dtype)]
        scratch = [pltpu.SemaphoreType.DMA((2, count - 1))] * 2
    else:
        rows //= count
        shapes = [jax.ShapeDtypeStruct((rows, width), jnp.float32)]
        scratch = [pltpu.VMEM((2, count, CHUNKS, rows // CHUNKS, width), jnp.bfloat16)] * 2
        scratch += [pltpu.SemaphoreType.DMA((2, count, CHUNKS))] * 2
    sizes.append(len(scratch))
    for weight, split in zip(weights, splits):
        operands.append(weight)
        shapes.append(jax.ShapeDtypeStruct(weight_shape(weight.shape, split), jnp.float32))
        more = weight_scratch(weight.shape, split, dp_count)
        sizes.append(len(more))
        scratch += more
    if vectors is not None:
        operands.append(vectors)
        shapes.append(jax.ShapeDtypeStruct(vectors.shape, vectors.dtype))
        levels = len(reduce_levels(dp_count))
        more = [
            pltpu.VMEM((levels,) + vectors.shape, vectors.dtype),
            pltpu.VMEM((levels,) + vectors.shape, vectors.dtype),
            pltpu.VMEM((count,) + vectors.shape, vectors.dtype),
            pltpu.SemaphoreType.DMA((levels + count,)),
            pltpu.SemaphoreType.DMA((levels + count,)),
        ]
        sizes.append(len(more))
        scratch += more
    results = pl.pallas_call(
        functools.partial(chain_kernel, kind, tuple(splits), shared, count, dp_count, tuple(sizes)),
        out_shape=shapes,
        in_specs=[pl.BlockSpec(memory_space=pltpu.VMEM)] * len(operands),
        out_specs=[pl.BlockSpec(memory_space=pltpu.VMEM)] * len(operands),
        scratch_shapes=scratch,
        compiler_params=pltpu.CompilerParams(
            collective_id=ident, has_side_effects=True, vmem_limit_bytes=VMEM_BYTES
        ),
        cost_estimate=pl.CostEstimate(
            flops=0, bytes_accessed=60 * 1024 * 1024, transcendentals=0
        ),
        name="chain_" + kind + str(ident),
    )(*operands)
    return results[0] if len(results) == 1 else results


def gather_tokens(block):
    return chain_call("gather", 0, block)


def scatter_tokens(part):
    return chain_call("scatter", 1, part)


def slot_moves(swap):
    col_count = lax.axis_size("col")
    half = col_count // 2
    pairs = []
    for row in range(2):
        for col in range(col_count):
            there = (col // half) * col_count + 2 * (col % half) + (row ^ swap)
            pairs.append((row * col_count + col, there))
    return pairs


def to_slot_rows(stored):
    row, col = lax.axis_index("row"), lax.axis_index("col")
    rows = stored.shape[0] // 2
    landed = []
    for swap in range(2):
        block = lax.dynamic_slice_in_dim(stored, (row ^ swap) * rows, rows, 0)
        landed.append(lax.ppermute(block, ("row", "col"), slot_moves(swap)))
    odd = (col % 2) == 1
    left = jnp.where(odd, landed[1], landed[0])
    right = jnp.where(odd, landed[0], landed[1])
    return jnp.concatenate([left, right], axis=1)


def from_slot_rows(block):
    row, col = lax.axis_index("row"), lax.axis_index("col")
    width = block.shape[1] // 2
    landed = []
    for swap in range(2):
        piece = lax.dynamic_slice_in_dim(block, ((col % 2) ^ swap) * width, width, 1)
        pairs = [(there, here) for here, there in slot_moves(swap)]
        landed.append(lax.ppermute(piece, ("row", "col"), pairs))
    upper = jnp.where(row == 1, landed[1], landed[0])
    lower = jnp.where(row == 1, landed[0], landed[1])
    return jnp.concatenate([upper, lower], axis=0)


def norm_forward(summed, gain_row, shift_row):
    average = jnp.mean(summed, axis=1, keepdims=True)
    centred = summed - average
    variance = jnp.mean(centred * centred, axis=1, keepdims=True)
    inverse = lax.rsqrt(variance + EPSILON)
    normal = centred * inverse
    return (normal * gain_row + shift_row, normal, inverse)


def norm_backward(upstream, normal, inverse, gain_row):
    scaled = upstream * gain_row
    average = jnp.mean(scaled, axis=1, keepdims=True)
    crossed = jnp.mean(scaled * normal, axis=1, keepdims=True)
    return (scaled - average - normal * crossed) * inverse


def slot_scores(query_part, key_part, length):
    scores = jnp.einsum(
        "qhd,khd->hqk", query_part, key_part, preferred_element_type=jnp.float32
    ) * HD ** (-0.5)
    valid_keys = lax.iota(jnp.int32, key_part.shape[0]) < length
    return jnp.where(valid_keys[None, None, :], scores, MASKED)


def slot_forward(slot_item):
    query_part, key_part, value_part, length = slot_item
    scores = slot_scores(query_part, key_part, length)
    row_top = jnp.max(scores, axis=2, keepdims=True)
    exponent = jnp.exp(scores - row_top)
    row_total = jnp.sum(exponent, axis=2, keepdims=True)
    probabilities = (exponent / row_total).astype(jnp.bfloat16)
    mixed = jnp.einsum(
        "hqk,khd->qhd", probabilities, value_part, preferred_element_type=jnp.float32
    )
    return (mixed.astype(jnp.bfloat16), (row_top + jnp.log(row_total))[:, :, 0])


def slot_backward(slot_item):
    query_part, key_part, value_part, length, logsum, grad_heads = slot_item
    probabilities = jnp.exp(slot_scores(query_part, key_part, length) - logsum[:, :, None])
    grad_probs = jnp.einsum(
        "qhd,khd->hqk", grad_heads, value_part, preferred_element_type=jnp.float32
    )
    grad_values = jnp.einsum(
        "hqk,qhd->khd",
        probabilities.astype(jnp.bfloat16),
        grad_heads,
        preferred_element_type=jnp.float32,
    )
    along = jnp.sum(probabilities * grad_probs, axis=2, keepdims=True)
    grad_scores = (probabilities * (grad_probs - along)).astype(jnp.bfloat16)
    grad_query = jnp.einsum(
        "hqk,khd->qhd", grad_scores, key_part, preferred_element_type=jnp.float32
    ) * HD ** (-0.5)
    grad_keys = jnp.einsum(
        "hqk,qhd->khd", grad_scores, query_part, preferred_element_type=jnp.float32
    ) * HD ** (-0.5)
    return jnp.stack([grad_query, grad_keys, grad_values], axis=2)


def both_halves(half, dimension):
    other = lax.ppermute(half, "row", [(0, 1), (1, 0)])
    ahead = lax.axis_index("row") == 0
    return jnp.concatenate(
        [jnp.where(ahead, half, other), jnp.where(ahead, other, half)], axis=dimension
    )


def per_device(
    layer_input,
    lengths,
    attend_weight,
    attend_bias,
    mixer_weight,
    mixer_bias,
    first_gain,
    first_shift,
    widen_weight,
    widen_bias,
    narrow_weight,
    narrow_bias,
    second_gain,
    second_shift,
    cotangent,
):
    row_rank = lax.axis_index("row")
    col_rank = lax.axis_index("col")
    heads_here = attend_bias.shape[0]
    input_block = to_slot_rows(layer_input)
    block_rows = input_block.shape[0]
    length = lax.dynamic_index_in_dim(lengths, row_rank, 0, keepdims=False)
    vectors = jnp.stack(
        [mixer_bias, first_gain, first_shift, narrow_bias, second_gain, second_shift]
    )
    vectors = both_halves(vectors, 1)
    mixer_bias, first_gain, first_shift, narrow_bias, second_gain, second_shift = vectors
    attend_weight = both_halves(attend_weight, 0)
    mixer_weight = both_halves(mixer_weight, 1)
    widen_weight = lax.all_gather(widen_weight, "row", axis=0, tiled=True)
    narrow_weight = lax.all_gather(narrow_weight, "row", axis=1, tiled=True)

    gathered_input = gather_tokens(input_block)
    slot_rows = gathered_input.shape[0]
    bias_full = jnp.concatenate(
        [attend_bias[:, :HD], jnp.zeros((heads_here, HD), jnp.float32), attend_bias[:, HD:]],
        axis=1,
    ).reshape(heads_here * 3 * HD)
    packed = (product(gathered_input, attend_weight) + bias_full).astype(jnp.bfloat16)
    split_heads = packed.reshape(slot_rows, heads_here, 3, HD)
    query_all = split_heads[:, :, 0]
    keys_all = split_heads[:, :, 1]
    values_all = split_heads[:, :, 2]
    mixed, logsum = slot_forward((query_all, keys_all, values_all, length))
    mixed_block = mixed.reshape(slot_rows, heads_here * HD)
    attended = scatter_tokens(product(mixed_block, mixer_weight)) + mixer_bias
    first_out, first_normal, first_inverse = norm_forward(
        input_block.astype(jnp.float32) + attended, first_gain, first_shift
    )
    gathered_first = gather_tokens(first_out.astype(jnp.bfloat16))
    widened = product(gathered_first, widen_weight) + widen_bias
    active, gelu_pull = jax.vjp(gelu_exact, widened)
    active_block = active.astype(jnp.bfloat16)
    narrowed = scatter_tokens(product(active_block, narrow_weight)) + narrow_bias
    second_out, second_normal, second_inverse = norm_forward(
        first_out + narrowed, second_gain, second_shift
    )
    layer_output = from_slot_rows(second_out.astype(jnp.bfloat16))
    positions = col_rank * block_rows + lax.iota(jnp.int32, block_rows)
    upstream = jnp.where(
        (positions < length)[:, None], to_slot_rows(cotangent).astype(jnp.float32), 0.0
    )
    second_gain_part = jnp.sum(upstream * second_normal, axis=0)
    second_shift_part = jnp.sum(upstream, axis=0)
    grad_second = norm_backward(upstream, second_normal, second_inverse, second_gain)
    grad_narrowed = grad_second.astype(jnp.bfloat16)
    narrow_bias_part = jnp.sum(grad_narrowed, axis=0, dtype=jnp.float32)
    grad_narrow_block = gather_tokens(grad_narrowed)
    narrow_part = inner_rows(active_block, grad_narrow_block).astype(jnp.bfloat16)
    grad_active = outer_back(grad_narrow_block, narrow_weight)
    grad_widened = gelu_pull(grad_active)[0].astype(jnp.bfloat16)
    widen_bias_part = jnp.sum(grad_widened, axis=0, dtype=jnp.float32)
    widen_part = inner_rows(gathered_first, grad_widened).astype(jnp.bfloat16)
    grad_first, narrow_total, widen_total = chain_call(
        "scatter",
        2,
        outer_back(grad_widened, widen_weight),
        (narrow_part, widen_part),
        (1, 0),
    )
    grad_first = grad_first + grad_second
    first_gain_part = jnp.sum(grad_first * first_normal, axis=0)
    first_shift_part = jnp.sum(grad_first, axis=0)
    grad_attended = norm_backward(grad_first, first_normal, first_inverse, first_gain)
    grad_mix = grad_attended.astype(jnp.bfloat16)
    mixer_bias_part = jnp.sum(grad_mix, axis=0, dtype=jnp.float32)
    grad_mixer_block = gather_tokens(grad_mix)
    mixer_part = inner_rows(grad_mixer_block, mixed_block).astype(jnp.bfloat16)
    grad_mixed = outer_back(grad_mixer_block, mixer_weight).astype(jnp.bfloat16)
    grad_heads = grad_mixed.reshape(slot_rows, heads_here, HD)
    grad_slots = slot_backward((query_all, keys_all, values_all, length, logsum, grad_heads))
    grad_packed = grad_slots.reshape(slot_rows, heads_here * 3 * HD).astype(jnp.bfloat16)
    packed_sums = jnp.sum(grad_packed, axis=0, dtype=jnp.float32).reshape(heads_here, 3, HD)
    attend_bias_part = jnp.concatenate([packed_sums[:, 0], packed_sums[:, 2]], axis=1)
    attend_part = inner_rows(gathered_input, grad_packed).astype(jnp.bfloat16)
    model = mixer_bias_part.shape[0]
    attend_bias_flat = attend_bias_part.reshape(-1)
    vector_parts = jnp.stack(
        [
            mixer_bias_part,
            first_gain_part,
            first_shift_part,
            narrow_bias_part,
            second_gain_part,
            second_shift_part,
            jnp.pad(widen_bias_part, (0, model - widen_bias_part.shape[0])),
            jnp.pad(attend_bias_flat, (0, model - attend_bias_flat.shape[0])),
        ]
    )
    input_gradient, attend_total, mixer_total, vector_sums = chain_call(
        "scatter",
        3,
        outer_back(grad_packed, attend_weight),
        (attend_part, mixer_part),
        (0, 0),
        vector_parts,
        6,
    )
    mixer_total = mixer_total.T
    input_gradient = from_slot_rows((input_gradient + grad_attended).astype(jnp.bfloat16))
    input_gradient = input_gradient.astype(jnp.float32)
    half = model // 2
    vector_totals = lax.dynamic_slice_in_dim(vector_sums, row_rank * half, half, 1)
    column_totals = (
        vector_sums[7, : attend_bias_flat.shape[0]].reshape(attend_bias_part.shape),
        vector_sums[6, : widen_bias_part.shape[0]],
    )
    return (
        layer_output,
        input_gradient,
        attend_total,
        column_totals[0],
        mixer_total,
        vector_totals[0],
        vector_totals[1],
        vector_totals[2],
        widen_total,
        column_totals[1],
        narrow_total,
        vector_totals[3],
        vector_totals[4],
        vector_totals[5],
    )


def solution(mesh):
    return jax.shard_map(
        per_device,
        mesh=mesh,
        in_specs=(
            P(("dp", "col"), "row"),
            P("dp"),
            P("row", "col"),
            P("col", None),
            P("col", "row"),
            P("row"),
            P("row"),
            P("row"),
            P("row", "col"),
            P("col"),
            P("col", "row"),
            P("row"),
            P("row"),
            P("row"),
            P(("dp", "col"), "row"),
        ),
        out_specs=(
            P(("dp", "col"), "row"),
            P(("dp", "col"), "row"),
            P("row", "col"),
            P("col", None),
            P("col", "row"),
            P("row"),
            P("row"),
            P("row"),
            P("row", "col"),
            P("col"),
            P("col", "row"),
            P("row"),
            P("row"),
            P("row"),
        ),
        check_vma=False,
    )
```

```python
import functools

import jax
import jax.numpy as jnp
from jax import lax
from jax.experimental import pallas as pl
from jax.experimental.pallas import tpu as pltpu
from jax.sharding import PartitionSpec as P

D = 1024
HD = 64


EPSILON = 1e-12
MASKED = -1e30


def product(left_side, right_side):
    return jnp.dot(left_side, right_side, preferred_element_type=jnp.float32)


def inner_rows(left_side, right_side):
    return lax.dot_general(
        left_side, right_side, (((0,), (0,)), ((), ())), preferred_element_type=jnp.float32
    )


def outer_back(left_side, right_side):
    return lax.dot_general(
        left_side, right_side, (((1,), (1,)), ((), ())), preferred_element_type=jnp.float32
    )


def gelu_exact(values):
    return jax.nn.gelu(values, approximate=False)


VMEM_BYTES = 48 * 1024 * 1024
MESH = pl.DeviceIdType.MESH
CHUNKS = 2


def reduce_levels(dp_count):
    levels = [("dp", 1), ("row", 1)]
    bit = 2
    while bit < dp_count:
        levels.append(("dp", bit))
        bit *= 2
    return levels


def greet(me, count, levels, whole_chain):
    barrier = pltpu.get_barrier_semaphore()
    for axis, bit in levels:
        pl.semaphore_signal(
            barrier, inc=1, device_id={axis: lax.axis_index(axis) ^ bit}, device_id_type=MESH
        )
    if whole_chain:
        for step in range(1, count):
            pl.semaphore_signal(
                barrier, inc=1, device_id={"col": lax.rem(me + step, count)}, device_id_type=MESH
            )
        pl.semaphore_wait(barrier, len(levels) + count - 1)
        return

    @pl.when(me > 0)
    def _():
        pl.semaphore_signal(barrier, inc=1, device_id={"col": me - 1}, device_id_type=MESH)

    @pl.when(me < count - 1)
    def _():
        pl.semaphore_signal(barrier, inc=1, device_id={"col": me + 1}, device_id_type=MESH)

    inner = (me > 0) & (me < count - 1)

    @pl.when(inner)
    def _():
        pl.semaphore_wait(barrier, len(levels) + 2)

    @pl.when(jnp.logical_not(inner))
    def _():
        pl.semaphore_wait(barrier, len(levels) + 1)


def gather_stages(count, block_ref, out_ref, send_sem, recv_sem):
    me = lax.axis_index("col")
    rows = block_ref.shape[0]

    def span(owner):
        return out_ref.at[pl.ds(pl.multiple_of(owner * rows, rows), rows)]

    def hop(source, owner, target, way, step):
        return pltpu.make_async_remote_copy(
            src_ref=source,
            dst_ref=span(owner),
            send_sem=send_sem.at[way, step],
            recv_sem=recv_sem.at[way, step],
            device_id={"col": target},
            device_id_type=MESH,
        )

    def start(step):
        @pl.when((me < count - 1) & (me - step >= 0))
        def _():
            source = block_ref if step == 0 else span(me - step)
            hop(source, me - step, me + 1, 0, step).start()

        @pl.when((me > 0) & (me + step <= count - 1))
        def _():
            source = block_ref if step == 0 else span(me + step)
            hop(source, me + step, me - 1, 1, step).start()

        if step == 0:
            out_ref[pl.ds(pl.multiple_of(me * rows, rows), rows), :] = block_ref[...]

    def arrive(step):
        @pl.when(me - step - 1 >= 0)
        def _():
            hop(span(me - step - 1), me - step - 1, me, 0, step).wait_recv()

        @pl.when(me + step + 1 <= count - 1)
        def _():
            hop(span(me + step + 1), me + step + 1, me, 1, step).wait_recv()

    def middle(step):
        arrive(step - 1)
        start(step)

    def last():
        arrive(count - 2)
        for step in range(count - 1):

            @pl.when((me < count - 1) & (me - step >= 0))
            def _():
                hop(span(me - step), me - step, me + 1, 0, step).wait_send()

            @pl.when((me > 0) & (me + step <= count - 1))
            def _():
                hop(span(me + step), me + step, me - 1, 1, step).wait_send()

    return (
        [functools.partial(start, 0)]
        + [functools.partial(middle, step) for step in range(1, count - 1)]
        + [last]
    )


def scatter_stages(count, part_ref, out_ref, held, sent, send_sem, recv_sem):
    me = lax.axis_index("col")
    rows = out_ref.shape[0] // CHUNKS

    def mine(owner, chunk):
        start = pl.multiple_of((owner * CHUNKS + chunk) * rows, rows)
        return part_ref[pl.ds(start, rows), :].astype(jnp.float32)

    def hop(way, owner, chunk, target):
        return pltpu.make_async_remote_copy(
            src_ref=sent.at[way, owner, chunk],
            dst_ref=held.at[way, owner, chunk],
            send_sem=send_sem.at[way, owner, chunk],
            recv_sem=recv_sem.at[way, owner, chunk],
            device_id={"col": target},
            device_id_type=MESH,
        )

    def flows(step):
        return (
            (0, count - 1 - step, me < count - 1 - step),
            (1, step, me > step),
        )

    def one(way, owner, inside, chunk):
        first = me == 0 if way == 0 else me == count - 1
        target = me + 1 if way == 0 else me - 1

        @pl.when(inside & first)
        def _():
            sent[way, owner, chunk] = mine(owner, chunk).astype(sent.dtype)
            hop(way, owner, chunk, target).start()

        @pl.when(inside & jnp.logical_not(first))
        def _():
            hop(way, owner, chunk, target).wait_recv()
            total = mine(owner, chunk) + held[way, owner, chunk].astype(jnp.float32)
            sent[way, owner, chunk] = total.astype(sent.dtype)
            hop(way, owner, chunk, target).start()

    def move(step):
        for chunk in range(CHUNKS):
            for way, owner, inside in flows(step):
                one(way, owner, inside, chunk)

    def last():
        for chunk in range(CHUNKS):
            place = pl.ds(chunk * rows, rows)
            out_ref[place, :] = mine(me, chunk)

            @pl.when(me > 0)
            def _():
                hop(0, me, chunk, me).wait_recv()
                out_ref[place, :] += held[0, me, chunk].astype(jnp.float32)

            @pl.when(me < count - 1)
            def _():
                hop(1, me, chunk, me).wait_recv()
                out_ref[place, :] += held[1, me, chunk].astype(jnp.float32)

        for step in range(count - 1):
            for way, owner, inside in flows(step):

                @pl.when(inside)
                def _():
                    for chunk in range(CHUNKS):
                        hop(way, owner, chunk, me).wait_send()

    return [functools.partial(move, step) for step in range(count - 1)] + [last]


def weight_shape(part_shape, split):
    rows, width = part_shape
    return (rows // 2, width) if split == 0 else (rows, width // 2)


def weight_scratch(part_shape, split, dp_count):
    rows, width = weight_shape(part_shape, split)
    count = len(reduce_levels(dp_count))
    half = rows // 2
    scratch = [
        pltpu.VMEM((2, half, width), jnp.bfloat16),
        pltpu.VMEM((half, width), jnp.bfloat16),
        pltpu.VMEM((half, width), jnp.bfloat16),
        pltpu.VMEM((half, width), jnp.float32),
        pltpu.VMEM((rows, width), jnp.bfloat16),
        pltpu.SemaphoreType.DMA((2 * count + 1,)),
        pltpu.SemaphoreType.DMA((2 * count + 1,)),
    ]
    for level in range(2, count):
        piece = half >> (level - 1)
        scratch += [pltpu.VMEM((piece, width), jnp.bfloat16)] * 2
    return scratch


def weight_stages(split, dp_count, part_ref, out_ref, scratch):
    near, toward, beside, total, whole, send_sem, recv_sem = scratch[:7]
    deeper = scratch[7:]
    levels = reduce_levels(dp_count)
    rows, width = out_ref.shape
    half = rows // 2
    dp, row = lax.axis_index("dp"), lax.axis_index("row")

    def at(side, start, size):
        if split == 0:
            return (pl.ds(pl.multiple_of(side * rows + start, size), size), slice(None))
        return (
            pl.ds(pl.multiple_of(start, size), size),
            pl.ds(pl.multiple_of(side * width, width), width),
        )

    def copy(source, landing, place, level):
        axis, bit = levels[level]
        return pltpu.make_async_remote_copy(
            src_ref=source,
            dst_ref=landing,
            send_sem=send_sem.at[place],
            recv_sem=recv_sem.at[place],
            device_id={axis: lax.axis_index(axis) ^ bit},
            device_id_type=MESH,
        )

    low = dp % 2
    core_copies = [
        copy(part_ref.at[at(side, (1 - low) * half, half)], near.at[place], place, 0)
        for place, side in ((0, 1 - row), (1, row))
    ]
    row_copy = copy(toward, beside, 2, 1)
    waits = core_copies + [row_copy]
    stages = []

    def begin():
        for item in core_copies:
            item.start()

    def summed(side, place):
        return part_ref[at(side, low * half, half)].astype(jnp.float32) + near[place].astype(
            jnp.float32
        )

    def core_done():
        core_copies[0].wait_recv()
        toward[...] = summed(1 - row, 0).astype(jnp.bfloat16)
        row_copy.start()
        core_copies[1].wait_recv()
        total[...] = summed(row, 1)

    kept, size = 0, half
    halvings = []
    for level in range(2, len(levels)):
        side = (dp // levels[level][1]) % 2
        size //= 2
        item = copy(deeper[2 * level - 4], deeper[2 * level - 3], level + 1, level)
        waits.append(item)
        halvings.append((level, item, kept + (1 - side) * size, kept + side * size, size))
        kept = kept + side * size

    def send_halving(entry):
        level, item, other, _, extent = entry
        deeper[2 * level - 4][...] = total[
            pl.ds(pl.multiple_of(other, extent), extent), :
        ].astype(jnp.bfloat16)
        item.start()

    def take_halving(entry):
        level, item, _, own, extent = entry
        item.wait_recv()
        place = pl.ds(pl.multiple_of(own, extent), extent)
        total[place, :] = total[place, :] + deeper[2 * level - 3][...].astype(jnp.float32)

    doublings = []
    start, extent = low * half + kept, size
    for level in list(range(len(levels) - 1, 1, -1)) + [0]:
        place = len(levels) + 1 + len(doublings)
        ref = whole.at[pl.ds(pl.multiple_of(start, extent), extent)]
        side = (dp // levels[level][1]) % 2
        item = copy(ref, ref, place, level)
        other = whole.at[
            pl.ds(pl.multiple_of(start + (1 - 2 * side) * extent, extent), extent)
        ]
        doublings.append((item, copy(other, other, place, level)))
        start, extent = start - side * extent, 2 * extent

    def start_doubling():
        own = pl.ds(pl.multiple_of(low * half + kept, size), size)
        whole[own, :] = total[pl.ds(pl.multiple_of(kept, size), size), :].astype(jnp.bfloat16)
        doublings[0][0].start()

    def row_done():
        row_copy.wait_recv()
        total[...] += beside[...].astype(jnp.float32)
        if halvings:
            send_halving(halvings[0])
        else:
            start_doubling()

    def halved(position):
        take_halving(halvings[position])
        if position + 1 < len(halvings):
            send_halving(halvings[position + 1])
        else:
            start_doubling()

    def doubled(position):
        doublings[position][1].wait_recv()
        if position + 1 < len(doublings):
            doublings[position + 1][0].start()
        else:
            out_ref[...] = whole[...].astype(jnp.float32)
            for item in waits:
                item.wait_send()
            for item, _ in doublings:
                item.wait_send()

    stages = [begin, core_done, row_done]
    stages += [functools.partial(halved, position) for position in range(len(halvings))]
    stages += [functools.partial(doubled, position) for position in range(len(doublings))]
    return stages


def vector_stages(count, dp_count, shared, part_ref, out_ref, totals, landed, across, send_sem, recv_sem):
    levels = reduce_levels(dp_count)
    me = lax.axis_index("col")

    def copy(level):
        axis, bit = levels[level]
        return pltpu.make_async_remote_copy(
            src_ref=part_ref if level == 0 else totals.at[level - 1],
            dst_ref=landed.at[level],
            send_sem=send_sem.at[level],
            recv_sem=recv_sem.at[level],
            device_id={axis: lax.axis_index(axis) ^ bit},
            device_id_type=MESH,
        )

    def spread(step):
        return pltpu.make_async_remote_copy(
            src_ref=totals.at[len(levels) - 1],
            dst_ref=across.at[me],
            send_sem=send_sem.at[len(levels) + step],
            recv_sem=recv_sem.at[len(levels) + step],
            device_id={"col": lax.rem(me + step, count)},
            device_id_type=MESH,
        )

    def arrival(step):
        return pltpu.make_async_remote_copy(
            src_ref=totals.at[len(levels) - 1],
            dst_ref=across.at[lax.rem(me - step + count, count)],
            send_sem=send_sem.at[len(levels) + step],
            recv_sem=recv_sem.at[len(levels) + step],
            device_id={"col": lax.rem(me + step, count)},
            device_id_type=MESH,
        )

    def take(level):
        copy(level).wait_recv()
        held = part_ref[...] if level == 0 else totals[level - 1]
        totals[level] = held + landed[level]
        if level + 1 < len(levels):
            copy(level + 1).start()
        else:
            across[me] = totals[level]
            for step in range(1, count):
                spread(step).start()

    def finish():
        for step in range(1, count):
            arrival(step).wait_recv()
        whole = across[0]
        for other in range(1, count):
            whole = whole + across[other]
        shared_rows = lax.broadcasted_iota(jnp.int32, whole.shape, 0) < shared
        out_ref[...] = jnp.where(shared_rows, whole, totals[len(levels) - 1])
        for level in range(len(levels)):
            copy(level).wait_send()
        for step in range(1, count):
            spread(step).wait_send()

    return (
        [lambda: copy(0).start()]
        + [functools.partial(take, level) for level in range(len(levels))]
        + [finish]
    )


def chain_kernel(kind, splits, shared, count, dp_count, sizes, *refs):
    me = lax.axis_index("col")
    refs = list(refs)

    def pull(number):
        taken = refs[:number]
        del refs[:number]
        return taken

    extras = len(splits) + (shared > 0)
    inputs, outputs = pull(1 + extras), pull(1 + extras)
    greet(me, count, reduce_levels(dp_count) if extras else [], shared > 0)
    lines = [
        (gather_stages if kind == "gather" else scatter_stages)(
            count, inputs[0], outputs[0], *pull(sizes[0])
        )
    ]
    for place, split in enumerate(splits):
        lines.append(
            weight_stages(
                split, dp_count, inputs[1 + place], outputs[1 + place], pull(sizes[1 + place])
            )
        )
    if shared > 0:
        lines.append(
            vector_stages(count, dp_count, shared, inputs[-1], outputs[-1], *pull(sizes[-1]))
        )
    for position in range(max(len(line) for line in lines)):
        for line in lines:
            if position < len(line):
                line[position]()


def chain_call(kind, ident, block, weights=(), splits=(), vectors=None, shared=0):
    count, dp_count = lax.axis_size("col"), lax.axis_size("dp")
    rows, width = block.shape
    operands, sizes = [block], []
    if kind == "gather":
        shapes = [jax.ShapeDtypeStruct((count * rows, width), block.dtype)]
        scratch = [pltpu.SemaphoreType.DMA((2, count - 1))] * 2
    else:
        rows //= count
        shapes = [jax.ShapeDtypeStruct((rows, width), jnp.float32)]
        scratch = [pltpu.VMEM((2, count, CHUNKS, rows // CHUNKS, width), jnp.bfloat16)] * 2
        scratch += [pltpu.SemaphoreType.DMA((2, count, CHUNKS))] * 2
    sizes.append(len(scratch))
    for weight, split in zip(weights, splits):
        operands.append(weight)
        shapes.append(jax.ShapeDtypeStruct(weight_shape(weight.shape, split), jnp.float32))
        more = weight_scratch(weight.shape, split, dp_count)
        sizes.append(len(more))
        scratch += more
    if vectors is not None:
        operands.append(vectors)
        shapes.append(jax.ShapeDtypeStruct(vectors.shape, vectors.dtype))
        levels = len(reduce_levels(dp_count))
        more = [
            pltpu.VMEM((levels,) + vectors.shape, vectors.dtype),
            pltpu.VMEM((levels,) + vectors.shape, vectors.dtype),
            pltpu.VMEM((count,) + vectors.shape, vectors.dtype),
            pltpu.SemaphoreType.DMA((levels + count,)),
            pltpu.SemaphoreType.DMA((levels + count,)),
        ]
        sizes.append(len(more))
        scratch += more
    results = pl.pallas_call(
        functools.partial(chain_kernel, kind, tuple(splits), shared, count, dp_count, tuple(sizes)),
        out_shape=shapes,
        in_specs=[pl.BlockSpec(memory_space=pltpu.VMEM)] * len(operands),
        out_specs=[pl.BlockSpec(memory_space=pltpu.VMEM)] * len(operands),
        scratch_shapes=scratch,
        compiler_params=pltpu.CompilerParams(
            collective_id=ident, has_side_effects=True, vmem_limit_bytes=VMEM_BYTES
        ),
        cost_estimate=pl.CostEstimate(
            flops=0, bytes_accessed=60 * 1024 * 1024, transcendentals=0
        ),
        name="chain_" + kind + str(ident),
    )(*operands)
    return results[0] if len(results) == 1 else results


def gather_tokens(block):
    return chain_call("gather", 0, block)


def scatter_tokens(part):
    return chain_call("scatter", 1, part)


def slot_moves(swap):
    col_count = lax.axis_size("col")
    half = col_count // 2
    pairs = []
    for row in range(2):
        for col in range(col_count):
            there = (col // half) * col_count + 2 * (col % half) + (row ^ swap)
            pairs.append((row * col_count + col, there))
    return pairs


def to_slot_rows(stored):
    row, col = lax.axis_index("row"), lax.axis_index("col")
    rows = stored.shape[0] // 2
    landed = []
    for swap in range(2):
        block = lax.dynamic_slice_in_dim(stored, (row ^ swap) * rows, rows, 0)
        landed.append(lax.ppermute(block, ("row", "col"), slot_moves(swap)))
    odd = (col % 2) == 1
    left = jnp.where(odd, landed[1], landed[0])
    right = jnp.where(odd, landed[0], landed[1])
    return jnp.concatenate([left, right], axis=1)


def from_slot_rows(block):
    row, col = lax.axis_index("row"), lax.axis_index("col")
    width = block.shape[1] // 2
    landed = []
    for swap in range(2):
        piece = lax.dynamic_slice_in_dim(block, ((col % 2) ^ swap) * width, width, 1)
        pairs = [(there, here) for here, there in slot_moves(swap)]
        landed.append(lax.ppermute(piece, ("row", "col"), pairs))
    upper = jnp.where(row == 1, landed[1], landed[0])
    lower = jnp.where(row == 1, landed[0], landed[1])
    return jnp.concatenate([upper, lower], axis=0)


def norm_forward(summed, gain_row, shift_row):
    average = jnp.mean(summed, axis=1, keepdims=True)
    centred = summed - average
    variance = jnp.mean(centred * centred, axis=1, keepdims=True)
    inverse = lax.rsqrt(variance + EPSILON)
    normal = centred * inverse
    return (normal * gain_row + shift_row, normal, inverse)


def norm_backward(upstream, normal, inverse, gain_row):
    scaled = upstream * gain_row
    average = jnp.mean(scaled, axis=1, keepdims=True)
    crossed = jnp.mean(scaled * normal, axis=1, keepdims=True)
    return (scaled - average - normal * crossed) * inverse


def slot_scores(query_part, key_part, length):
    scores = jnp.einsum(
        "qhd,khd->hqk", query_part, key_part, preferred_element_type=jnp.float32
    ) * HD ** (-0.5)
    valid_keys = lax.iota(jnp.int32, key_part.shape[0]) < length
    return jnp.where(valid_keys[None, None, :], scores, MASKED)


def slot_forward(slot_item):
    query_part, key_part, value_part, length = slot_item
    scores = slot_scores(query_part, key_part, length)
    row_top = jnp.max(scores, axis=2, keepdims=True)
    exponent = jnp.exp(scores - row_top)
    row_total = jnp.sum(exponent, axis=2, keepdims=True)
    probabilities = (exponent / row_total).astype(jnp.bfloat16)
    mixed = jnp.einsum(
        "hqk,khd->qhd", probabilities, value_part, preferred_element_type=jnp.float32
    )
    return (mixed.astype(jnp.bfloat16), (row_top + jnp.log(row_total))[:, :, 0])


def slot_backward(slot_item):
    query_part, key_part, value_part, length, logsum, grad_heads = slot_item
    probabilities = jnp.exp(slot_scores(query_part, key_part, length) - logsum[:, :, None])
    grad_probs = jnp.einsum(
        "qhd,khd->hqk", grad_heads, value_part, preferred_element_type=jnp.float32
    )
    grad_values = jnp.einsum(
        "hqk,qhd->khd",
        probabilities.astype(jnp.bfloat16),
        grad_heads,
        preferred_element_type=jnp.float32,
    )
    along = jnp.sum(probabilities * grad_probs, axis=2, keepdims=True)
    grad_scores = (probabilities * (grad_probs - along)).astype(jnp.bfloat16)
    grad_query = jnp.einsum(
        "hqk,khd->qhd", grad_scores, key_part, preferred_element_type=jnp.float32
    ) * HD ** (-0.5)
    grad_keys = jnp.einsum(
        "hqk,qhd->khd", grad_scores, query_part, preferred_element_type=jnp.float32
    ) * HD ** (-0.5)
    return jnp.stack([grad_query, grad_keys, grad_values], axis=2)


def both_halves(half, dimension):
    other = lax.ppermute(half, "row", [(0, 1), (1, 0)])
    ahead = lax.axis_index("row") == 0
    return jnp.concatenate(
        [jnp.where(ahead, half, other), jnp.where(ahead, other, half)], axis=dimension
    )


def per_device(
    layer_input,
    lengths,
    attend_weight,
    attend_bias,
    mixer_weight,
    mixer_bias,
    first_gain,
    first_shift,
    widen_weight,
    widen_bias,
    narrow_weight,
    narrow_bias,
    second_gain,
    second_shift,
    cotangent,
):
    row_rank = lax.axis_index("row")
    col_rank = lax.axis_index("col")
    heads_here = attend_bias.shape[0]
    input_block = to_slot_rows(layer_input)
    block_rows = input_block.shape[0]
    length = lax.dynamic_index_in_dim(lengths, row_rank, 0, keepdims=False)
    vectors = jnp.stack(
        [mixer_bias, first_gain, first_shift, narrow_bias, second_gain, second_shift]
    )
    vectors = both_halves(vectors, 1)
    mixer_bias, first_gain, first_shift, narrow_bias, second_gain, second_shift = vectors
    attend_weight = both_halves(attend_weight, 0)
    mixer_weight = both_halves(mixer_weight, 1)
    input_block, widen_weight, narrow_weight = lax.optimization_barrier(
        (input_block, widen_weight, narrow_weight)
    )
    widen_weight = lax.all_gather(widen_weight, "row", axis=0, tiled=True)
    narrow_weight = lax.all_gather(narrow_weight, "row", axis=1, tiled=True)

    gathered_input = gather_tokens(input_block)
    slot_rows = gathered_input.shape[0]
    bias_full = jnp.concatenate(
        [attend_bias[:, :HD], jnp.zeros((heads_here, HD), jnp.float32), attend_bias[:, HD:]],
        axis=1,
    ).reshape(heads_here * 3 * HD)
    packed = (product(gathered_input, attend_weight) + bias_full).astype(jnp.bfloat16)
    split_heads = packed.reshape(slot_rows, heads_here, 3, HD)
    query_all = split_heads[:, :, 0]
    keys_all = split_heads[:, :, 1]
    values_all = split_heads[:, :, 2]
    mixed, logsum = slot_forward((query_all, keys_all, values_all, length))
    mixed_block = mixed.reshape(slot_rows, heads_here * HD)
    attended = scatter_tokens(product(mixed_block, mixer_weight)) + mixer_bias
    first_out, first_normal, first_inverse = norm_forward(
        input_block.astype(jnp.float32) + attended, first_gain, first_shift
    )
    gathered_first = gather_tokens(first_out.astype(jnp.bfloat16))
    widened = product(gathered_first, widen_weight) + widen_bias
    active, gelu_pull = jax.vjp(gelu_exact, widened)
    active_block = active.astype(jnp.bfloat16)
    narrowed = scatter_tokens(product(active_block, narrow_weight)) + narrow_bias
    second_out, second_normal, second_inverse = norm_forward(
        first_out + narrowed, second_gain, second_shift
    )
    layer_output = from_slot_rows(second_out.astype(jnp.bfloat16))
    positions = col_rank * block_rows + lax.iota(jnp.int32, block_rows)
    upstream = jnp.where(
        (positions < length)[:, None], to_slot_rows(cotangent).astype(jnp.float32), 0.0
    )
    second_gain_part = jnp.sum(upstream * second_normal, axis=0)
    second_shift_part = jnp.sum(upstream, axis=0)
    grad_second = norm_backward(upstream, second_normal, second_inverse, second_gain)
    grad_narrowed = grad_second.astype(jnp.bfloat16)
    narrow_bias_part = jnp.sum(grad_narrowed, axis=0, dtype=jnp.float32)
    grad_narrow_block = gather_tokens(grad_narrowed)
    narrow_part = inner_rows(active_block, grad_narrow_block).astype(jnp.bfloat16)
    grad_active = outer_back(grad_narrow_block, narrow_weight)
    grad_widened = gelu_pull(grad_active)[0].astype(jnp.bfloat16)
    widen_bias_part = jnp.sum(grad_widened, axis=0, dtype=jnp.float32)
    widen_part = inner_rows(gathered_first, grad_widened).astype(jnp.bfloat16)
    grad_first, narrow_total, widen_total = chain_call(
        "scatter",
        2,
        outer_back(grad_widened, widen_weight),
        (narrow_part, widen_part),
        (1, 0),
    )
    grad_first = grad_first + grad_second
    first_gain_part = jnp.sum(grad_first * first_normal, axis=0)
    first_shift_part = jnp.sum(grad_first, axis=0)
    grad_attended = norm_backward(grad_first, first_normal, first_inverse, first_gain)
    grad_mix = grad_attended.astype(jnp.bfloat16)
    mixer_bias_part = jnp.sum(grad_mix, axis=0, dtype=jnp.float32)
    grad_mixer_block = gather_tokens(grad_mix)
    mixer_part = inner_rows(grad_mixer_block, mixed_block).astype(jnp.bfloat16)
    grad_mixed = outer_back(grad_mixer_block, mixer_weight).astype(jnp.bfloat16)
    grad_heads = grad_mixed.reshape(slot_rows, heads_here, HD)
    grad_slots = slot_backward((query_all, keys_all, values_all, length, logsum, grad_heads))
    grad_packed = grad_slots.reshape(slot_rows, heads_here * 3 * HD).astype(jnp.bfloat16)
    packed_sums = jnp.sum(grad_packed, axis=0, dtype=jnp.float32).reshape(heads_here, 3, HD)
    attend_bias_part = jnp.concatenate([packed_sums[:, 0], packed_sums[:, 2]], axis=1)
    attend_part = inner_rows(gathered_input, grad_packed).astype(jnp.bfloat16)
    model = mixer_bias_part.shape[0]
    attend_bias_flat = attend_bias_part.reshape(-1)
    vector_parts = jnp.stack(
        [
            mixer_bias_part,
            first_gain_part,
            first_shift_part,
            narrow_bias_part,
            second_gain_part,
            second_shift_part,
            jnp.pad(widen_bias_part, (0, model - widen_bias_part.shape[0])),
            jnp.pad(attend_bias_flat, (0, model - attend_bias_flat.shape[0])),
        ]
    )
    input_gradient, attend_total, mixer_total, vector_sums = chain_call(
        "scatter",
        3,
        outer_back(grad_packed, attend_weight),
        (attend_part, mixer_part),
        (0, 0),
        vector_parts,
        6,
    )
    mixer_total = mixer_total.T
    input_gradient = from_slot_rows((input_gradient + grad_attended).astype(jnp.bfloat16))
    input_gradient = input_gradient.astype(jnp.float32)
    half = model // 2
    vector_totals = lax.dynamic_slice_in_dim(vector_sums, row_rank * half, half, 1)
    column_totals = (
        vector_sums[7, : attend_bias_flat.shape[0]].reshape(attend_bias_part.shape),
        vector_sums[6, : widen_bias_part.shape[0]],
    )
    return (
        layer_output,
        input_gradient,
        attend_total,
        column_totals[0],
        mixer_total,
        vector_totals[0],
        vector_totals[1],
        vector_totals[2],
        widen_total,
        column_totals[1],
        narrow_total,
        vector_totals[3],
        vector_totals[4],
        vector_totals[5],
    )


def solution(mesh):
    return jax.shard_map(
        per_device,
        mesh=mesh,
        in_specs=(
            P(("dp", "col"), "row"),
            P("dp"),
            P("row", "col"),
            P("col", None),
            P("col", "row"),
            P("row"),
            P("row"),
            P("row"),
            P("row", "col"),
            P("col"),
            P("col", "row"),
            P("row"),
            P("row"),
            P("row"),
            P(("dp", "col"), "row"),
        ),
        out_specs=(
            P(("dp", "col"), "row"),
            P(("dp", "col"), "row"),
            P("row", "col"),
            P("col", None),
            P("col", "row"),
            P("row"),
            P("row"),
            P("row"),
            P("row", "col"),
            P("col"),
            P("col", "row"),
            P("row"),
            P("row"),
            P("row"),
        ),
        check_vma=False,
    )
```
